256 devices in a mesh: param: 8 (over z_hi, core), slab: 8 (over x, z_lo), tile: 4 (over y).
Axes of the slice: x: 4, y: 4, z: 8 (z_hi: 4, z_lo: 2; z = z_hi * 2 + z_lo), core: 2. Of those that a mesh axis runs over, the one named last changes fastest.
Arguments:
- state: float32 [14, 24, 128, 128], P(None, 'slab', 'tile', 'param'), may hold values from 0 to 1
- sensitivity: float32 [64, 14, 24, 128, 128], P('param', None, 'slab', 'tile'), may hold values from -6 to 6
- packing: float32 [24, 128, 128], P('slab', 'tile'), may hold values from 0.5 to 2
- cell_zone: int32 [24, 128, 128], P('slab', 'tile'), may hold values from 0 to 7
- coefficients: float32 [8, 8], replicated, may hold values from 0.3 to 1.5
- param_target: int32 [64], P('param'), may hold values from 0 to 63
Outputs:
- new_state: float32 [14, 24, 128, 128], P(None, 'slab', 'tile', 'param')
- new_sensitivity: float32 [64, 14, 24, 128, 128], P('param', None, 'slab', 'tile')
The draws below stay inside these ranges and needn't reach their ends.
Inputs may be any that keep to these rules, and one draw needn't show every extreme that they name: param_target[p] // 8 is the kind and param_target[p] % 8 the zone of parameter p.
All inputs are finite; a program needn't handle non-finite values.
Results may differ from the reference program's by a relative error of at most 0.0003.
Values sent between devices are 32-bit elements; how exact they have to be, the bound alone decides.
A program may use at most 128 MiB of HBM per device.

```python
import math
import jax
import jax.numpy as jnp
from jax import lax

KINDS = 8
ZONES = 8
VARS = 14
NZ = 128
PARAMS = 64
NX = 24
NY = 128


def with_ends(entries, rng, low, high):
    dims = entries.shape
    index_at = [jax.random.randint(jax.random.fold_in(rng, axis), (), 0, dims[axis]) for axis in range(len(dims))]
    entries = entries.at[tuple(index_at)].set(low)
    longest = dims.index(max(dims))
    index_at[longest] = (index_at[longest] + 1) % dims[longest]
    return entries.at[tuple(index_at)].set(high)


def block_levels(stream_key, extent, shards, smallest, high):
    loudness = 1.0
    for dim, parts in shards:
        heights = jax.random.uniform(jax.random.fold_in(jax.random.fold_in(stream_key, 6), dim), (parts,), jnp.float32, smallest / len(shards), high / len(shards))
        loudness = loudness * jnp.repeat(jnp.exp(heights), extent[dim] // parts).reshape((-1,) + (1,) * (len(extent) - 1 - dim))
    return loudness


def gaussian(stream_key, shape, scale, reach, pieces=(), kind=jnp.bfloat16):
    drawn = jax.random.normal(stream_key, shape, jnp.float32) * scale
    if len(pieces) > 0:
        drawn = block_levels(stream_key, shape, pieces, -0.22, 0.18) * drawn
    return jnp.clip(drawn, min=-reach, max=reach).astype(kind)


def setup_inputs(seed: int = 0) -> dict:
    streams_of = jax.random.split(jax.random.key(seed), 7)
    return {
        "state": jnp.clip(1.0 * jax.random.uniform(streams_of[0], (VARS, NX, NY, NZ), jnp.float32) ** block_levels(streams_of[0], (VARS, NX, NY, NZ), ((1, 8), (2, 4), (3, 8)), -0.2, 0.2), 0.0, 1.0),
        "sensitivity": gaussian(streams_of[1], (PARAMS, VARS, NX, NY, NZ), 1.0, 6.0, ((0, 8), (2, 8), (3, 4)), jnp.float32),
        "packing": jnp.clip(jnp.exp(math.log(2.0) - 1.3862944 * jax.random.uniform(streams_of[2], (NX, NY, NZ), jnp.float32) ** block_levels(streams_of[2], (NX, NY, NZ), ((0, 8), (1, 4)), -0.2, 0.2)), 0.5, 2.0),
        "cell_zone": with_ends(jax.random.randint(streams_of[3], (NX, NY, NZ), 0, ZONES), jax.random.fold_in(streams_of[3], 1), 0, ZONES - 1).astype(jnp.int32),
        "coefficients": jnp.clip(jnp.exp(jax.random.uniform(streams_of[4], (KINDS, ZONES), jnp.float32, math.log(0.3), math.log(1.5))), 0.3, 1.5),
        "param_target": with_ends(jax.random.randint(streams_of[5], (PARAMS,), 0, KINDS * ZONES), jax.random.fold_in(streams_of[5], 1), 0, (KINDS * ZONES) - 1).astype(jnp.int32),
    }


STEP_LENGTH = 0.15
AXIAL_MIX = 0.5
RADIAL_MIX = 0.25
VELOCITY = 1.0
FILM_SCALE = 1.5
SHELL_WEIGHTS = (0.3, 0.6, 0.9, 1.2, 1.5)


def field_slice(values, lower_end, upper_end):
    return values[..., lower_end:upper_end, :, :, :]


def transport(padded):
    center = padded[..., 1:-1, 1:-1, :]
    widths = [(0, 0)] * (center.ndim - 1) + [(1, 1)]
    column = jnp.pad(center, widths)
    behind = padded[..., :-2, 1:-1, :]
    ahead = padded[..., 2:, 1:-1, :]
    lower_row = padded[..., 1:-1, :-2, :]
    upper_row = padded[..., 1:-1, 2:, :]
    axial = AXIAL_MIX * (ahead + behind - 2.0 * center)
    radial = RADIAL_MIX * (lower_row + upper_row + column[..., 2:] + column[..., :-2] - 4.0 * center)
    return axial + radial - VELOCITY * (center - behind)


def bulk_rate(padded, outer_shell, film_rate, packing):
    center = padded[..., 1:-1, 1:-1, :]
    return transport(padded) - film_rate * packing * (center - outer_shell)


def bulk_tangent(tangent_padded, tangent_outer, tangent_film, bulk_conc, outer_shell, film_rate, packing):
    tangent_center = tangent_padded[..., 1:-1, 1:-1, :]
    return transport(tangent_padded) - (tangent_film * packing * (bulk_conc - outer_shell) + film_rate * packing * (tangent_center - tangent_outer))


def shell_flux(shells):
    fluxes = [SHELL_WEIGHTS[shell_index] * (field_slice(shells, shell_index + 1, shell_index + 2) - field_slice(shells, shell_index, shell_index + 1)) for shell_index in range(5)]
    shell_rows = [fluxes[0]] + [fluxes[shell_index] - fluxes[shell_index - 1] for shell_index in range(1, 5)] + [-fluxes[4]]
    return jnp.concatenate(shell_rows, axis=-4)


def pellet_rate(bulk_conc, pore_one, pore_two, theta_field):
    denominator = 1.0 + field_slice(theta_field, 6, 7) * pore_one + field_slice(theta_field, 7, 8) * pore_two
    result_parts = []
    for component, pore_conc in ((0, pore_one), (1, pore_two)):
        film_rate = field_slice(theta_field, component, component + 1)
        diffusion = field_slice(theta_field, 2 + component, 3 + component)
        capacity = field_slice(theta_field, 4 + component, 5 + component)
        affinity = field_slice(theta_field, 6 + component, 7 + component)
        change = diffusion * shell_flux(pore_conc) - capacity * affinity * pore_conc / denominator
        surface = FILM_SCALE * film_rate * (field_slice(bulk_conc, component, component + 1) - field_slice(pore_conc, 5, 6))
        result_parts.append(field_slice(change, 0, 5))
        result_parts.append(field_slice(change, 5, 6) + surface)
    return jnp.concatenate(result_parts, axis=-4)


def pellet_tangent(bulk_conc, pore_one, pore_two, theta_field, tangent_bulk, tangent_one, tangent_two, tangent_theta):
    denominator = 1.0 + field_slice(theta_field, 6, 7) * pore_one + field_slice(theta_field, 7, 8) * pore_two
    tangent_denominator = (field_slice(theta_field, 6, 7) * tangent_one + pore_one * field_slice(tangent_theta, 6, 7)
                           + field_slice(theta_field, 7, 8) * tangent_two + pore_two * field_slice(tangent_theta, 7, 8))
    result_parts = []
    for component, pore_conc, tangent_pore in ((0, pore_one, tangent_one), (1, pore_two, tangent_two)):
        film_rate = field_slice(theta_field, component, component + 1)
        diffusion = field_slice(theta_field, 2 + component, 3 + component)
        capacity = field_slice(theta_field, 4 + component, 5 + component)
        affinity = field_slice(theta_field, 6 + component, 7 + component)
        tangent_film = field_slice(tangent_theta, component, component + 1)
        tangent_diffusion = field_slice(tangent_theta, 2 + component, 3 + component)
        tangent_capacity = field_slice(tangent_theta, 4 + component, 5 + component)
        tangent_affinity = field_slice(tangent_theta, 6 + component, 7 + component)
        uptake_tangent = ((tangent_capacity * affinity * pore_conc + capacity * tangent_affinity * pore_conc + capacity * affinity * tangent_pore) / denominator
                          - capacity * affinity * pore_conc * tangent_denominator / (denominator * denominator))
        change = tangent_diffusion * shell_flux(pore_conc) + diffusion * shell_flux(tangent_pore) - uptake_tangent
        surface = FILM_SCALE * (tangent_film * (field_slice(bulk_conc, component, component + 1) - field_slice(pore_conc, 5, 6))
                                + film_rate * (field_slice(tangent_bulk, component, component + 1) - field_slice(tangent_pore, 5, 6)))
        result_parts.append(field_slice(change, 0, 5))
        result_parts.append(field_slice(change, 5, 6) + surface)
    return jnp.concatenate(result_parts, axis=-4)


def zone_lookup(table, zones):
    result = jnp.zeros((table.shape[0],) + zones.shape, table.dtype)
    for zone_index in range(table.shape[1]):
        result = jnp.where(zones[None] == zone_index, table[:, zone_index][:, None, None, None], result)
    return result


def zone_tangents(targets, zones, kind_count, zone_count):
    kind_of = targets // zone_count
    zone_of = targets % zone_count
    chosen = (kind_of[:, None] == jnp.arange(kind_count)[None, :]).astype(jnp.float32)
    within = (zones[None] == zone_of[:, None, None, None]).astype(jnp.float32)
    return chosen[:, :, None, None, None] * within[:, None]


def outer_shells(values):
    return jnp.concatenate([field_slice(values, 7, 8), field_slice(values, 13, 14)], axis=-4)


def advance_state(padded, state_now, theta_field, packing):
    bulk_conc = field_slice(state_now, 0, 2)
    new_bulk = bulk_conc + STEP_LENGTH * bulk_rate(padded, outer_shells(state_now), field_slice(theta_field, 0, 2), packing)
    new_pores = field_slice(state_now, 2, 14) + STEP_LENGTH * pellet_rate(bulk_conc, field_slice(state_now, 2, 8), field_slice(state_now, 8, 14), theta_field)
    return jnp.concatenate([new_bulk, new_pores], axis=-4)


def advance_tangent(tangent_padded, tangent_now, state_now, theta_field, tangent_theta, packing):
    bulk_conc = field_slice(state_now, 0, 2)
    new_bulk = field_slice(tangent_now, 0, 2) + STEP_LENGTH * bulk_tangent(
        tangent_padded, outer_shells(tangent_now), field_slice(tangent_theta, 0, 2),
        bulk_conc, outer_shells(state_now), field_slice(theta_field, 0, 2), packing)
    new_pores = field_slice(tangent_now, 2, 14) + STEP_LENGTH * pellet_tangent(
        bulk_conc, field_slice(state_now, 2, 8), field_slice(state_now, 8, 14), theta_field,
        field_slice(tangent_now, 0, 2), field_slice(tangent_now, 2, 8), field_slice(tangent_now, 8, 14), tangent_theta)
    return jnp.concatenate([new_bulk, new_pores], axis=-4)


def pad_rim(values):
    return jnp.pad(values, ((0, 0), (1, 1), (1, 1), (0, 0)))


def reference(state, sensitivity, packing, cell_zone, coefficients, param_target):
    theta_field = zone_lookup(coefficients, cell_zone)
    history = [state]
    current = state
    for time_index in range(2):
        current = advance_state(pad_rim(field_slice(current, 0, 2)), current, theta_field, packing)
        history.append(current)

    def one_param(operands):
        tangent_now, target_value = operands
        tangent_theta = zone_tangents(target_value[None], cell_zone, KINDS, ZONES)[0]
        for time_index in range(2):
            tangent_now = advance_tangent(pad_rim(field_slice(tangent_now, 0, 2)), tangent_now, history[time_index], theta_field, tangent_theta, packing)
        return tangent_now

    return current, lax.map(one_param, (sensitivity, param_target))
```

```python
import jax
import jax.numpy as jnp
from jax import lax
from jax.experimental import pallas as pl
from jax.experimental.pallas import tpu as pltpu
from jax.sharding import PartitionSpec as P

DT = 0.15
AHEAD = DT * 0.5
BEHIND = DT * 1.5
SIDE = DT * 0.25
CENTER = 1.0 - DT * 3.0
FILM = DT * 1.5
G = (0.3, 0.6, 0.9, 1.2, 1.5)
F32 = jnp.float32

NP = 8
NB = 12
NG = 12

X0 = 0
X1 = X0 + 8
HS = X1 + 16
RS = HS + 2
Y0 = RS + 2
Y0S = Y0 + 2
Y1 = Y0S + 2
GA = Y1 + 18
GB = GA + 9
MESSAGES = GB + 7


def kernel(
    st_in, sens, pack, zone, coef, targ, st_out, out,
    sv, gst, hsend, hrecv, rsend, rrecv, turn,
    s0, s1, s2, th, ev, kv, pc, av, bv, gv,
    hx0, hx1, bb, bs, c1, p51, yb0, yr0, yb1, yr1,
    ss, rs, lsem,
):
    me, sl, ti = (lax.axis_index(a) for a in ("param", "slab", "tile"))
    h, c = lax.div(me, 2), lax.rem(me, 2)
    jp = lax.rem(h + 1, 4) * 2 + c
    jm = lax.rem(h + 3, 4) * 2 + c
    jo = lax.rem(h + 2, 4) * 2 + c
    other = 1 - 2 * c
    has_dn, has_up = sl > 0, sl < 7
    has_lo, has_hi = ti > 0, ti < 3
    up, dn = (me, sl + 1, ti), (me, sl - 1, ti)
    hi, lo = (me, sl, ti + 1), (me, sl, ti - 1)
    right, left, sib = (jp, sl, ti), (jm, sl, ti), (me + other, sl, ti)

    def loop(n, body):
        lax.fori_loop(0, n, lambda i, carry: (body(i), carry)[1], 0)

    def remote(src, dst, number, device):
        return pltpu.make_async_remote_copy(
            src_ref=src, dst_ref=dst, send_sem=ss.at[number], recv_sem=rs.at[number],
            device_id=device, device_id_type=pl.DeviceIdType.MESH,
        )

    bulk_copy = pltpu.make_async_copy(sens.at[:, pl.ds(0, 2)], sv.at[:, pl.ds(0, 2)], lsem.at[NP])
    bulk_copy.start()

    def shell_copy(p):
        return pltpu.make_async_copy(
            sens.at[p, pl.ds(2, 12)], sv.at[p, pl.ds(2, 12)], lsem.at[p]
        )

    loop(NP, lambda p: shell_copy(p).start())

    mine = pl.multiple_of(me * 16, 16)
    blank = jnp.zeros((16, 32), F32)
    for g in range(11):
        parts = [st_in[4 * g + k] if 4 * g + k < 42 else blank for k in range(4)]
        gst[g, pl.ds(mine, 16), :] = jnp.concatenate(parts, axis=-1)
    hsend[...] = jnp.concatenate([st_in[q] for q in (2, 5, 0, 3)], axis=-1)

    barrier = pltpu.get_barrier_semaphore()

    def greet(device):
        pl.semaphore_signal(barrier, inc=1, device_id=device, device_id_type=pl.DeviceIdType.MESH)

    for device in (right, left, sib):
        greet(device)
    for present, device in ((has_up, up), (has_dn, dn), (has_hi, hi), (has_lo, lo)):
        pl.when(present)(lambda device=device: greet(device))
    present_count = sum(x.astype(jnp.int32) for x in (has_up, has_dn, has_hi, has_lo))
    pl.semaphore_wait(barrier, 3 + present_count)

    class Pair:
        def __init__(self, number, srcs, dsts, slab):
            plus, minus = (up, dn) if slab else (hi, lo)
            self.to_plus, self.to_minus = (has_up, has_dn) if slab else (has_hi, has_lo)
            self.a = remote(srcs[0], dsts[0], number, plus)
            self.b = remote(srcs[1], dsts[1], number + 1, minus)

        def start(self):
            pl.when(self.to_plus)(lambda: self.a.start())
            pl.when(self.to_minus)(lambda: self.b.start())

        def wait_recv(self):
            pl.when(self.to_minus)(lambda: self.a.wait_recv())
            pl.when(self.to_plus)(lambda: self.b.wait_recv())

        def wait_send(self):
            pl.when(self.to_plus)(lambda: self.a.wait_send())
            pl.when(self.to_minus)(lambda: self.b.wait_send())

    halo_state = Pair(HS, (hsend, hsend), (hrecv.at[0], hrecv.at[1]), True)

    def halo0(k):
        two, bulk = pl.ds(2 * k, 2), pl.ds(0, 2)
        return Pair(
            X0 + 2 * k,
            (sens.at[two, bulk, pl.ds(8, 4)], sens.at[two, bulk, pl.ds(0, 4)]),
            (hx0.at[0, two], hx0.at[1, two]),
            True,
        )

    def halo1(p):
        return Pair(
            X1 + 2 * p,
            (bb.at[p, :, pl.ds(8, 4)], bb.at[p, :, pl.ds(0, 4)]),
            (hx1.at[0, p], hx1.at[1, p]),
            True,
        )

    partial_state = Pair(RS, (rsend, rsend), (rrecv.at[0], rrecv.at[1]), True)
    eight = pl.ds(0, NP)
    rows0 = Pair(Y0, (yb0.at[0, eight], yb0.at[1, eight]), (yr0.at[0, eight], yr0.at[1, eight]), False)
    rows0s = Pair(Y0S, (yb0.at[0, NP], yb0.at[1, NP]), (yr0.at[0, NP], yr0.at[1, NP]), False)

    def rows1(q):
        return Pair(Y1 + 2 * q, (yb1.at[0, q], yb1.at[1, q]), (yr1.at[0, q], yr1.at[1, q]), False)

    def shard(j, first, count):
        return gst.at[pl.ds(first, count), pl.ds(pl.multiple_of(j * 16, 16), 16)]

    def pass_on(j, first, count, number, device):
        ref = shard(j, first, count)
        return remote(ref, ref, number, device)

    send_a = [
        pass_on(me, 0, 11, GA, right), pass_on(me, 0, 11, GA + 1, left), pass_on(me, 0, 11, GA + 2, sib),
        pass_on(jm, 0, 6, GA + 3, right), pass_on(jm, 0, 11, GA + 4, sib),
        pass_on(jp, 6, 5, GA + 5, left), pass_on(jp, 0, 11, GA + 6, sib),
        pass_on(jo, 0, 6, GA + 7, sib), pass_on(jo, 6, 5, GA + 8, sib),
    ]
    recv_a = [
        pass_on(jm, 0, 11, GA, right), pass_on(jp, 0, 11, GA + 1, left), pass_on(me + other, 0, 11, GA + 2, sib),
        pass_on(jo, 0, 6, GA + 3, right), pass_on(jm + other, 0, 11, GA + 4, sib),
        pass_on(jo, 6, 5, GA + 5, left), pass_on(jp + other, 0, 11, GA + 6, sib),
        pass_on(jo + other, 0, 6, GA + 7, sib), pass_on(jo + other, 6, 5, GA + 8, sib),
    ]
    send_b = [
        pass_on(me, 11, 1, GB, right), pass_on(me, 11, 1, GB + 1, left), pass_on(me, 11, 1, GB + 2, sib),
        pass_on(jm, 11, 1, GB + 3, right), pass_on(jm, 11, 1, GB + 4, sib),
        pass_on(jp, 11, 1, GB + 5, sib), pass_on(jo, 11, 1, GB + 6, sib),
    ]
    recv_b = [
        pass_on(jm, 11, 1, GB, right), pass_on(jp, 11, 1, GB + 1, left), pass_on(me + other, 11, 1, GB + 2, sib),
        pass_on(jo, 11, 1, GB + 3, right), pass_on(jm + other, 11, 1, GB + 4, sib),
        pass_on(jp + other, 11, 1, GB + 5, sib), pass_on(jo + other, 11, 1, GB + 6, sib),
    ]

    halo_state.start()
    for k in range(3):
        send_a[k].start()
    loop(4, lambda k: halo0(k).start())

    def clear(ref, k):
        ref[k] = jnp.zeros(ref.shape[1:], F32)

    for absent, k in ((jnp.logical_not(has_dn), 0), (jnp.logical_not(has_up), 1)):
        @pl.when(absent)
        def _(k=k):
            for ref in (hrecv, rrecv):
                clear(ref, k)
            def one(p):
                hx0[k, p] = jnp.zeros(hx0.shape[2:], F32)
                hx1[k, p] = jnp.zeros(hx1.shape[2:], F32)
            loop(NP, one)
    for absent, k in ((jnp.logical_not(has_lo), 0), (jnp.logical_not(has_hi), 1)):
        @pl.when(absent)
        def _(k=k):
            clear(yr0, k)
            clear(yr1, k)

    def cell_theta(b):
        z = zone[b]
        is_zone = [z == j for j in range(1, 8)]
        values = []
        for k in range(8):
            v = jnp.full((8, 128), coef[k, 0], F32)
            for j in range(1, 8):
                v = jnp.where(is_zone[j - 1], coef[k, j], v)
            th[b, k] = v
            values.append(v)
        for i in range(2):
            exchange = DT * values[i] * pack[b]
            kv[i, b] = exchange
            pc[i, b] = CENTER - exchange
            for s in range(5):
                ev[b, 5 * i + s] = (DT * G[s]) * values[2 + i]

    loop(NB, cell_theta)

    bulk_copy.wait()

    def pack_rows0(p):
        for i in range(2):
            for x in range(3):
                r = 3 * i + x
                yb0[0, p, pl.ds(r, 1), :] = sv[p, i, 4 * x + 3, pl.ds(7, 1), :]
                yb0[1, p, pl.ds(r, 1), :] = sv[p, i, 4 * x, pl.ds(0, 1), :]

    loop(NP, pack_rows0)
    rows0.start()

    lane16 = lax.broadcasted_iota(jnp.int32, (16, 128), 1)
    halo_state.wait_recv()
    gst[11, pl.ds(mine, 16), :] = jnp.where(lane16 < 64, hrecv[0], hrecv[1])
    for k in range(3):
        send_b[k].start()
    recv_a[0].wait_recv()
    send_a[3].start()
    send_a[4].start()
    recv_a[1].wait_recv()
    send_a[5].start()
    send_a[6].start()
    recv_b[0].wait_recv()
    send_b[3].start()
    send_b[4].start()
    recv_b[1].wait_recv()
    send_b[5].start()
    recv_a[3].wait_recv()
    send_a[7].start()
    recv_a[5].wait_recv()
    send_a[8].start()
    recv_b[3].wait_recv()
    send_b[6].start()
    for k in (2, 4, 6, 7, 8):
        recv_a[k].wait_recv()
    for k in (2, 4, 5, 6):
        recv_b[k].wait_recv()

    def unpack(g):
        s0[pl.ds(16 * g, 16)] = gst[g].T.reshape(16, 8, 128)

    loop(NG, unpack)

    def state_rows(state, buffer):
        for i in range(2):
            for x in range(3):
                r = 3 * i + x
                buffer[0, NP, pl.ds(r, 1), :] = state[i * NB + 4 * x + 3, pl.ds(7, 1), :]
                buffer[1, NP, pl.ds(r, 1), :] = state[i * NB + 4 * x, pl.ds(0, 1), :]

    state_rows(s0, yb0)
    rows0s.start()

    def zero_tables(b):
        for n in range(2):
            gv[n, b] = jnp.zeros(gv.shape[2:], F32)

    loop(NB, zero_tables)

    def tables(n, now, later):
        def block(b):
            kf, dp, qm, bb_ = ([th[b, 2 * k + i] for i in range(2)] for k in range(4))
            conc = [now[i * NB + b] for i in range(2)]
            pore = [[now[(2 + 6 * i + s) * NB + b] for s in range(6)] for i in range(2)]
            cap = [qm[i] * bb_[i] for i in range(2)]
            film = [FILM * kf[i] for i in range(2)]
            for s in range(6):
                inverse = 1.0 / (1.0 + bb_[0] * pore[0][s] + bb_[1] * pore[1][s])
                u = [pore[i][s] * inverse for i in range(2)]
                for i in range(2):
                    f = 2 + 6 * i + s
                    rate = DT * cap[i] * inverse
                    kept = 1.0 - bb_[i] * u[i]
                    own = 1.0 - rate * kept
                    if s == 5:
                        own = own - film[i]
                    av[n, b, 6 * i + s] = own
                    bv[n, b, 6 * i + s] = rate * u[i] * bb_[1 - i]
                    if s == 0:
                        flux = G[0] * (pore[i][1] - pore[i][0])
                    elif s == 5:
                        flux = -(G[4] * (pore[i][5] - pore[i][4]))
                    else:
                        flux = G[s] * (pore[i][s + 1] - pore[i][s]) - G[s - 1] * (pore[i][s] - pore[i][s - 1])
                    gv[n, b, 2 + i, f] = DT * flux
                    gv[n, b, 4 + i, f] = -(DT * bb_[i]) * u[i]
                    gv[n, b, 6 + i, f] = -(DT * qm[i]) * u[i] * kept
                    gv[n, b, 7 - i, f] = DT * cap[i] * u[i] * u[1 - i]
                    fresh = pore[i][s] + DT * dp[i] * flux - DT * cap[i] * u[i]
                    if s == 5:
                        gap = conc[i] - pore[i][5]
                        gv[n, b, i, f] = FILM * gap
                        gv[n, b, i, i] = -(DT * pack[b]) * gap
                        fresh = fresh + film[i] * gap
                    later[f * NB + b] = fresh

        loop(NB, block)

    tables(0, s0, s1)

    row = lax.broadcasted_iota(jnp.int32, (32, 128), 0)
    lane = lax.broadcasted_iota(jnp.int32, (32, 128), 1)

    def around(v, below, above):
        return (
            jnp.where(row == 0, below, pltpu.roll(v, 1, 0))
            + jnp.where(row == 31, above, pltpu.roll(v, 31, 0))
            + jnp.where(lane == 0, 0.0, pltpu.roll(v, 1, 1))
            + jnp.where(lane == 127, 0.0, pltpu.roll(v, 127, 1))
        )

    def plane(values):
        return values.reshape(32, 128)

    def advance(i, planes, outer, below, above):
        result = []
        for x in range(3):
            four = pl.ds(4 * x, 4)
            v = planes[x]
            w = plane(pc[i, four]) * v + plane(kv[i, four]) * plane(outer(x)) + SIDE * around(v, below(x), above(x))
            if x > 0:
                w = w + BEHIND * planes[x - 1]
            if x < 2:
                w = w + AHEAD * planes[x + 1]
            result.append(w)
        return result

    def forcing(n, p, i, x):
        t = targ[p]
        four = pl.ds(4 * x, 4)
        return jnp.where(zone[four] == lax.rem(t, 8), gv[n, four, lax.div(t, 8), i], 0.0).reshape(32, 128)

    rows0.wait_recv()

    def partial(p):
        for i in range(2):
            planes = [plane(sv[p, i, pl.ds(4 * x, 4)]) for x in range(3)]
            fresh = advance(
                i, planes, lambda x: sv[p, 7 + 6 * i, pl.ds(4 * x, 4)],
                lambda x: yr0[0, p, pl.ds(3 * i + x, 1), :], lambda x: yr0[1, p, pl.ds(3 * i + x, 1), :],
            )
            for x in range(3):
                bb[p, i, pl.ds(4 * x, 4)] = (fresh[x] + forcing(0, p, i, x)).reshape(4, 8, 128)

    def partial_and_send(p):
        shell_copy(p).wait()
        partial(p)
        halo1(p).start()

    loop(NP, partial_and_send)

    rows0s.wait_recv()
    for i in range(2):
        planes = [plane(s0[pl.ds(i * NB + 4 * x, 4)]) for x in range(3)]
        fresh = advance(
            i, planes, lambda x: s0[pl.ds((7 + 6 * i) * NB + 4 * x, 4)],
            lambda x: yr0[0, NP, pl.ds(3 * i + x, 1), :], lambda x: yr0[1, NP, pl.ds(3 * i + x, 1), :],
        )
        bs[pl.ds(4 * i, 4)] = fresh[2].reshape(4, 8, 128)
        bs[pl.ds(8 + 4 * i, 4)] = fresh[0].reshape(4, 8, 128)
        s1[pl.ds(i * NB, 4)] = fresh[0].reshape(4, 8, 128) + BEHIND * s0[pl.ds(176 + 4 * i, 4)]
        s1[pl.ds(i * NB + 4, 4)] = fresh[1].reshape(4, 8, 128)
        s1[pl.ds(i * NB + 8, 4)] = fresh[2].reshape(4, 8, 128) + AHEAD * s0[pl.ds(184 + 4 * i, 4)]
    state_rows(s1, yb1)
    rows1(NP).start()
    turn[...] = bs[...].reshape(128, 128).T
    rsend[...] = turn[pl.ds(mine, 16), :]
    partial_state.start()
    tables(1, s1, s2)

    def whole(p):
        for i in range(2):
            c1[p, i, pl.ds(0, 4)] = bb[p, i, pl.ds(0, 4)] + BEHIND * hx0[0, p, i]
            c1[p, i, pl.ds(4, 4)] = bb[p, i, pl.ds(4, 4)]
            c1[p, i, pl.ds(8, 4)] = bb[p, i, pl.ds(8, 4)] + AHEAD * hx0[1, p, i]
            for x in range(3):
                r = 3 * i + x
                yb1[0, p, pl.ds(r, 1), :] = c1[p, i, 4 * x + 3, pl.ds(7, 1), :]
                yb1[1, p, pl.ds(r, 1), :] = c1[p, i, 4 * x, pl.ds(0, 1), :]
        rows1(p).start()

    def shells(p):
        t = targ[p]
        kind, target_zone = lax.div(t, 8), lax.rem(t, 8)

        def block(b):
            within = zone[b] == target_zone
            t_now = [[sv[p, 2 + 6 * i + s, b] for s in range(6)] for i in range(2)]
            for n in range(2):
                bulk = sv if n == 0 else c1
                t_later = []
                for i in range(2):
                    flux = [ev[b, 5 * i + s] * (t_now[i][s + 1] - t_now[i][s]) for s in range(5)]
                    fresh = []
                    for s in range(6):
                        v = av[n, b, 6 * i + s] * t_now[i][s] + bv[n, b, 6 * i + s] * t_now[1 - i][s]
                        if s < 5:
                            v = v + flux[s]
                        if s > 0:
                            v = v - flux[s - 1]
                        if s == 5:
                            v = v + FILM * th[b, i] * bulk[p, i, b]
                        fresh.append(v + jnp.where(within, gv[n, b, kind, 2 + 6 * i + s], 0.0))
                    t_later.append(fresh)
                t_now = t_later
                if n == 0:
                    for i in range(2):
                        p51[p, i, b] = t_now[i][5]
            for i in range(2):
                for s in range(6):
                    out[p, 2 + 6 * i + s, b] = t_now[i][s]

        loop(NB, block)

    def step_chunk(k):
        halo0(k).wait_recv()
        for j in range(2):
            whole(2 * k + j)
        loop(2, lambda j: shells(2 * k + j))

    loop(4, step_chunk)

    from_dn = (BEHIND * AHEAD) * has_dn.astype(F32)
    from_up = (BEHIND * AHEAD) * has_up.astype(F32)

    def second(p):
        rows1(p).wait_recv()
        for i in range(2):
            planes = [plane(c1[p, i, pl.ds(4 * x, 4)]) for x in range(3)]
            fresh = advance(
                i, planes, lambda x: p51[p, i, pl.ds(4 * x, 4)],
                lambda x: yr1[0, p, pl.ds(3 * i + x, 1), :], lambda x: yr1[1, p, pl.ds(3 * i + x, 1), :],
            )
            fresh[0] = fresh[0] + from_dn * plane(sv[p, i, pl.ds(0, 4)])
            fresh[2] = fresh[2] + from_up * plane(sv[p, i, pl.ds(8, 4)])
            for x in range(3):
                out[p, i, pl.ds(4 * x, 4)] = (fresh[x] + forcing(1, p, i, x)).reshape(4, 8, 128)

    loop(NP, second)

    rows1(NP).wait_recv()
    for i in range(2):
        planes = [plane(s1[pl.ds(i * NB + 4 * x, 4)]) for x in range(3)]
        fresh = advance(
            i, planes, lambda x: s1[pl.ds((7 + 6 * i) * NB + 4 * x, 4)],
            lambda x: yr1[0, NP, pl.ds(3 * i + x, 1), :], lambda x: yr1[1, NP, pl.ds(3 * i + x, 1), :],
        )
        fresh[0] = fresh[0] + from_dn * plane(s0[pl.ds(i * NB, 4)])
        fresh[2] = fresh[2] + from_up * plane(s0[pl.ds(i * NB + 8, 4)])
        for x in range(3):
            s2[pl.ds(i * NB + 4 * x, 4)] = fresh[x].reshape(4, 8, 128)
    partial_state.wait_recv()
    merged = jnp.where(lane16 < 64, rrecv[0], rrecv[1])
    rolled = pltpu.roll(merged, 64, 1)
    for g in range(11):
        turn[...] = s2[pl.ds(16 * g, 16)].reshape(128, 128).T
        own = turn[pl.ds(mine, 16), :]
        if g == 0:
            own = own + jnp.where(lane16 < 32, BEHIND * merged, 0.0)
            own = own + jnp.where(lane16 >= 96, BEHIND * rolled, jnp.where(lane16 >= 64, AHEAD * merged, 0.0))
        if g == 1:
            own = own + jnp.where((lane16 >= 32) & (lane16 < 64), AHEAD * rolled, 0.0)
        for k in range(4):
            if 4 * g + k < 42:
                st_out[4 * g + k] = own[:, 32 * k : 32 * k + 32]

    def last(p):
        halo1(p).wait_recv()
        for i in range(2):
            out[p, i, pl.ds(0, 4)] = out[p, i, pl.ds(0, 4)] + BEHIND * hx1[0, p, i]
            out[p, i, pl.ds(8, 4)] = out[p, i, pl.ds(8, 4)] + AHEAD * hx1[1, p, i]

    loop(NP, last)

    halo_state.wait_send()
    partial_state.wait_send()
    rows0.wait_send()
    rows0s.wait_send()
    loop(4, lambda k: halo0(k).wait_send())
    loop(NP, lambda p: halo1(p).wait_send())
    loop(NP + 1, lambda q: rows1(q).wait_send())
    for message in send_a + send_b:
        message.wait_send()


def shards(state, sensitivity, packing, cell_zone, coefficients, param_target):
    packed = jnp.transpose(state, (0, 1, 3, 2)).reshape(42, 16, 32)
    vmem = pl.BlockSpec(memory_space=pltpu.VMEM)
    smem = pl.BlockSpec(memory_space=pltpu.SMEM)
    anywhere = pl.BlockSpec(memory_space=pl.ANY)
    scratch = [
        (NP, 14, NB, 8, 128),
        (NG, 128, 128),
        (16, 128), (2, 16, 128), (16, 128), (2, 16, 128), (128, 128),
        (192, 8, 128), (168, 8, 128), (176, 8, 128),
        (NB, 8, 8, 128), (NB, 10, 8, 128), (2, NB, 8, 128), (2, NB, 8, 128),
        (2, NB, 12, 8, 128), (2, NB, 12, 8, 128), (2, NB, 8, 14, 8, 128),
        (2, NP, 2, 4, 8, 128), (2, NP, 2, 4, 8, 128),
        (NP, 2, NB, 8, 128), (16, 8, 128), (NP, 2, NB, 8, 128), (NP, 2, NB, 8, 128),
        (2, NP + 1, 8, 128), (2, NP + 1, 8, 128), (2, NP + 1, 8, 128), (2, NP + 1, 8, 128),
    ]
    new_state, new_sens = pl.pallas_call(
        kernel,
        out_shape=(
            jax.ShapeDtypeStruct((42, 16, 32), F32),
            jax.ShapeDtypeStruct((NP, 14, NB, 8, 128), F32),
        ),
        in_specs=[vmem, anywhere, vmem, vmem, smem, smem],
        out_specs=(vmem, vmem),
        scratch_shapes=[pltpu.VMEM(shape, F32) for shape in scratch]
        + [
            pltpu.SemaphoreType.DMA((MESSAGES,)),
            pltpu.SemaphoreType.DMA((MESSAGES,)),
            pltpu.SemaphoreType.DMA((NP + 1,)),
        ],
        compiler_params=pltpu.CompilerParams(
            collective_id=0, has_side_effects=True, vmem_limit_bytes=46 * 1024 * 1024
        ),
        name="column",
    )(
        packed,
        sensitivity.reshape(NP, 14, NB, 8, 128),
        packing.reshape(NB, 8, 128),
        cell_zone.reshape(NB, 8, 128),
        coefficients,
        param_target,
    )
    new_state = jnp.transpose(new_state.reshape(14, 3, 16, 32), (0, 1, 3, 2))
    return new_state, new_sens.reshape(NP, 14, 3, 32, 128)


def solution(mesh):
    placed = (
        P(None, "slab", "tile", "param"),
        P("param", None, "slab", "tile", None),
        P("slab", "tile", None),
        P("slab", "tile", None),
        P(),
        P("param"),
    )
    return jax.shard_map(
        shards,
        mesh=mesh,
        in_specs=placed,
        out_specs=(P(None, "slab", "tile", "param"), P("param", None, "slab", "tile", None)),
        check_vma=False,
    )
```

```python
import jax
import jax.numpy as jnp
from jax import lax
from jax.experimental import pallas as pl
from jax.experimental.pallas import tpu as pltpu
from jax.sharding import PartitionSpec as P

DT = 0.15
AHEAD = DT * 0.5
BEHIND = DT * 1.5
SIDE = DT * 0.25
CENTER = 1.0 - DT * 3.0
FILM = DT * 1.5
G = (0.3, 0.6, 0.9, 1.2, 1.5)
F32 = jnp.float32

NP = 8
NB = 12
NG = 13

X0 = 0
X1 = X0 + 8
HS = X1 + 16
RS = HS + 2
Y0 = RS + 2
YS = Y0 + 2
Y1 = YS + 2
GA = Y1 + 18
GB = GA + 9
GW = GB + 7
MESSAGES = GW + 7
SMALL = NP + 1
LOCAL = SMALL + 5


def kernel(
    st_arg, sens, pack_arg, zone_arg, coef_arg, targ_arg, st_out, out,
    sv, gst, wst, hsend, hrecv, tile_recv, rsend, rrecv, turn,
    s0, s1, s2, th, ev, kv, pc, av, bv, gv, gp, fw,
    hx0, hx1, bb, bs, c1, p51, yb0, yr0, yb1, yr1,
    st_in, pack, zone, coef, targ,
    ss, rs, lsem,
):
    me, sl, ti = (lax.axis_index(a) for a in ("param", "slab", "tile"))
    h, c = lax.div(me, 2), lax.rem(me, 2)
    jp = lax.rem(h + 1, 4) * 2 + c
    jm = lax.rem(h + 3, 4) * 2 + c
    jo = lax.rem(h + 2, 4) * 2 + c
    other = 1 - 2 * c
    has_dn, has_up = sl > 0, sl < 7
    has_lo, has_hi = ti > 0, ti < 3
    up, dn = (me, sl + 1, ti), (me, sl - 1, ti)
    hi, lo = (me, sl, ti + 1), (me, sl, ti - 1)
    right, left, across, sib = (jp, sl, ti), (jm, sl, ti), (jo, sl, ti), (me + other, sl, ti)

    def loop(n, body):
        lax.fori_loop(0, n, lambda i, carry: (body(i), carry)[1], 0)

    def remote(src, dst, number, device):
        return pltpu.make_async_remote_copy(
            src_ref=src, dst_ref=dst, send_sem=ss.at[number], recv_sem=rs.at[number],
            device_id=device, device_id_type=pl.DeviceIdType.MESH,
        )

    barrier = pltpu.get_barrier_semaphore()

    def greet(device):
        pl.semaphore_signal(barrier, inc=1, device_id=device, device_id_type=pl.DeviceIdType.MESH)

    for device in (right, left, across, sib):
        greet(device)
    for present, device in ((has_up, up), (has_dn, dn), (has_hi, hi), (has_lo, lo)):
        pl.when(present)(lambda device=device: greet(device))
    present_count = sum(x.astype(jnp.int32) for x in (has_up, has_dn, has_hi, has_lo))

    bulk_copy = pltpu.make_async_copy(sens.at[:, pl.ds(0, 2)], sv.at[:, pl.ds(0, 2)], lsem.at[NP])

    def shell_copy(p):
        return pltpu.make_async_copy(
            sens.at[p, pl.ds(2, 12)], sv.at[p, pl.ds(2, 12)], lsem.at[p]
        )

    small = [
        pltpu.make_async_copy(src, dst, lsem.at[SMALL + k])
        for k, (src, dst) in enumerate(
            ((st_arg, st_in), (pack_arg, pack), (zone_arg, zone), (coef_arg, coef), (targ_arg, targ))
        )
    ]
    for copy in small:
        copy.start()
    bulk_copy.start()
    loop(NP, lambda p: shell_copy(p).start())
    small[0].wait()

    mine = pl.multiple_of(me * 16, 16)
    blank = jnp.zeros((16, 32), F32)
    for g in range(11):
        parts = [st_in[4 * g + k] if 4 * g + k < 42 else blank for k in range(4)]
        gst[g, pl.ds(mine, 16), :] = jnp.concatenate(parts, axis=-1)
    hsend[...] = jnp.concatenate([st_in[q] for q in (2, 5, 0, 3)], axis=-1)
    wst[pl.ds(mine, 16), :] = jnp.concatenate(
        [st_in[q] - st_in[r] for q, r in ((0, 21), (3, 39), (2, 23), (5, 41))], axis=-1
    )
    for copy in small[1:]:
        copy.wait()

    def zero_tables(b):
        nothing = jnp.zeros((8, 128), F32)
        for n in range(2):
            for k in range(6):
                for f in range(12):
                    if k < 2 and f == 6 * k + 5 or k >= 2 and f // 6 == k % 2:
                        continue
                    gv[n, b, k, f] = nothing

    loop(NB, zero_tables)

    pl.semaphore_wait(barrier, 4 + present_count)

    class Pair:
        def __init__(self, number, srcs, dsts, slab):
            plus, minus = (up, dn) if slab else (hi, lo)
            self.to_plus, self.to_minus = (has_up, has_dn) if slab else (has_hi, has_lo)
            self.a = remote(srcs[0], dsts[0], number, plus)
            self.b = remote(srcs[1], dsts[1], number + 1, minus)

        def start(self):
            pl.when(self.to_plus)(lambda: self.a.start())
            pl.when(self.to_minus)(lambda: self.b.start())

        def wait_recv(self):
            pl.when(self.to_minus)(lambda: self.a.wait_recv())
            pl.when(self.to_plus)(lambda: self.b.wait_recv())

        def wait_send(self):
            pl.when(self.to_plus)(lambda: self.a.wait_send())
            pl.when(self.to_minus)(lambda: self.b.wait_send())

    halo_state = Pair(HS, (hsend, hsend), (hrecv.at[0], hrecv.at[1]), True)

    def halo0(k):
        two, bulk = pl.ds(2 * k, 2), pl.ds(0, 2)
        return Pair(
            X0 + 2 * k,
            (sens.at[two, bulk, pl.ds(8, 4)], sens.at[two, bulk, pl.ds(0, 4)]),
            (hx0.at[0, two], hx0.at[1, two]),
            True,
        )

    def halo1(p):
        return Pair(
            X1 + 2 * p,
            (bb.at[p, :, pl.ds(8, 4)], bb.at[p, :, pl.ds(0, 4)]),
            (hx1.at[0, p], hx1.at[1, p]),
            True,
        )

    partial_state = Pair(RS, (rsend, rsend), (rrecv.at[0], rrecv.at[1]), True)
    eight = pl.ds(0, NP)
    rows0 = Pair(Y0, (yb0.at[0, eight], yb0.at[1, eight]), (yr0.at[0, eight], yr0.at[1, eight]), False)

    def rows1(q):
        return Pair(Y1 + 2 * q, (yb1.at[0, q], yb1.at[1, q]), (yr1.at[0, q], yr1.at[1, q]), False)

    def shard(j, first, count):
        return gst.at[pl.ds(first, count), pl.ds(pl.multiple_of(j * 16, 16), 16)]

    def pass_on(j, first, count, number, device):
        ref = shard(j, first, count)
        return remote(ref, ref, number, device)

    send_a = [
        pass_on(me, 0, 11, GA, right), pass_on(me, 0, 11, GA + 1, left), pass_on(me, 0, 11, GA + 2, sib),
        pass_on(jm, 0, 6, GA + 3, right), pass_on(jm, 0, 11, GA + 4, sib),
        pass_on(jp, 6, 5, GA + 5, left), pass_on(jp, 0, 11, GA + 6, sib),
        pass_on(jo, 0, 6, GA + 7, sib), pass_on(jo, 6, 5, GA + 8, sib),
    ]
    recv_a = [
        pass_on(jm, 0, 11, GA, right), pass_on(jp, 0, 11, GA + 1, left), pass_on(me + other, 0, 11, GA + 2, sib),
        pass_on(jo, 0, 6, GA + 3, right), pass_on(jm + other, 0, 11, GA + 4, sib),
        pass_on(jo, 6, 5, GA + 5, left), pass_on(jp + other, 0, 11, GA + 6, sib),
        pass_on(jo + other, 0, 6, GA + 7, sib), pass_on(jo + other, 6, 5, GA + 8, sib),
    ]
    tile_state = Pair(YS, (shard(me, 0, 2), shard(me, 0, 2)), (tile_recv.at[0], tile_recv.at[1]), False)

    def small_gather(ref_of, number):
        def messages(shards):
            devices = (right, left, across, sib, sib, sib, sib)
            return [
                remote(ref_of(j), ref_of(j), number + k, device)
                for k, (j, device) in enumerate(zip(shards, devices))
            ]

        return (
            messages((me, me, me, me, jm, jp, jo)),
            messages((jm, jp, jo, me + other, jm + other, jp + other, jo + other)),
        )

    send_b, recv_b = small_gather(lambda j: shard(j, 11, 2), GB)
    send_w, recv_w = small_gather(lambda j: wst.at[pl.ds(pl.multiple_of(j * 16, 16), 16)], GW)

    for k in range(4):
        send_w[k].start()
    halo_state.start()
    tile_state.start()
    for k in range(3):
        send_a[k].start()
    loop(4, lambda k: halo0(k).start())

    def clear(ref, k):
        ref[k] = jnp.zeros(ref.shape[1:], F32)

    for absent, k in ((jnp.logical_not(has_dn), 0), (jnp.logical_not(has_up), 1)):
        @pl.when(absent)
        def _(k=k):
            for ref in (hrecv, rrecv):
                clear(ref, k)
            def one(p):
                hx0[k, p] = jnp.zeros(hx0.shape[2:], F32)
                hx1[k, p] = jnp.zeros(hx1.shape[2:], F32)
            loop(NP, one)
    for absent, k in ((jnp.logical_not(has_lo), 0), (jnp.logical_not(has_hi), 1)):
        @pl.when(absent)
        def _(k=k):
            for ref in (yr0, yr1, tile_recv):
                clear(ref, k)

    def cell_theta(b):
        z = zone[b]
        is_zone = [z == j for j in range(1, 8)]
        values = []
        for k in range(8):
            v = jnp.full((8, 128), coef[k, 0], F32)
            for j in range(1, 8):
                v = jnp.where(is_zone[j - 1], coef[k, j], v)
            th[b, k] = v
            values.append(v)
        for i in range(2):
            exchange = DT * values[i] * pack[b]
            kv[i, b] = exchange
            pc[i, b] = CENTER - exchange
            for s in range(5):
                ev[b, 5 * i + s] = (DT * G[s]) * values[2 + i]

    loop(NB, cell_theta)

    bulk_copy.wait()

    def pack_rows0(p):
        for i in range(2):
            for x in range(3):
                r = 3 * i + x
                yb0[0, p, pl.ds(r, 1), :] = sv[p, i, 4 * x + 3, pl.ds(7, 1), :]
                yb0[1, p, pl.ds(r, 1), :] = sv[p, i, 4 * x, pl.ds(0, 1), :]

    loop(NP, pack_rows0)
    rows0.start()

    lane16 = lax.broadcasted_iota(jnp.int32, (16, 128), 1)
    halo_state.wait_recv()
    gst[11, pl.ds(mine, 16), :] = jnp.where(lane16 < 64, hrecv[0], hrecv[1])
    tile_state.wait_recv()
    spot = lax.rem(lane16, 32)
    gst[12, pl.ds(mine, 16), :] = jnp.where(
        spot == 31,
        tile_recv[0, 0],
        jnp.where(
            spot == 0,
            tile_recv[1, 0],
            jnp.where(spot == 30, pltpu.roll(tile_recv[0, 1], 127, 1), pltpu.roll(tile_recv[1, 1], 1, 1)),
        ),
    )
    for k in range(4):
        send_b[k].start()
    for k in range(3):
        recv_w[k].wait_recv()
        send_w[4 + k].start()
    recv_a[0].wait_recv()
    send_a[3].start()
    send_a[4].start()
    recv_a[1].wait_recv()
    send_a[5].start()
    send_a[6].start()

    row = lax.broadcasted_iota(jnp.int32, (32, 128), 0)
    lane = lax.broadcasted_iota(jnp.int32, (32, 128), 1)

    def around(v, below, above):
        return (
            jnp.where(row == 0, below, pltpu.roll(v, 1, 0))
            + jnp.where(row == 31, above, pltpu.roll(v, 31, 0))
            + jnp.where(lane == 0, 0.0, pltpu.roll(v, 1, 1))
            + jnp.where(lane == 127, 0.0, pltpu.roll(v, 127, 1))
        )

    def plane(values):
        return values.reshape(32, 128)

    def advance(i, planes, outer, below, above):
        result = []
        for x in range(3):
            four = pl.ds(4 * x, 4)
            v = planes[x]
            w = plane(pc[i, four]) * v + plane(kv[i, four]) * plane(outer(x)) + SIDE * around(v, below(x), above(x))
            if x > 0:
                w = w + BEHIND * planes[x - 1]
            if x < 2:
                w = w + AHEAD * planes[x + 1]
            result.append(w)
        return result

    def forcing(p, i, x, values):
        t = targ[p]
        target = jnp.where(lax.div(t, 8) == i, lax.rem(t, 8), -1)
        return jnp.where(zone[pl.ds(4 * x, 4)] == target, values, 0.0)

    for k in range(3, 7):
        recv_w[k].wait_recv()
    turned = wst[...].T.reshape(2, 2, 4, 8, 128)
    for k in range(2):
        for i in range(2):
            fw[k, i] = -(DT * pack[pl.ds(8 * k, 4)]) * turned[k, i]
    rows0.wait_recv()

    def partial_and_send(p):
        shell_copy(p).wait()
        for i in range(2):
            planes = [plane(sv[p, i, pl.ds(4 * x, 4)]) for x in range(3)]
            fresh = advance(
                i, planes, lambda x: sv[p, 7 + 6 * i, pl.ds(4 * x, 4)],
                lambda x: yr0[0, p, pl.ds(3 * i + x, 1), :], lambda x: yr0[1, p, pl.ds(3 * i + x, 1), :],
            )
            for x in range(3):
                v = fresh[x].reshape(4, 8, 128)
                if x != 1:
                    v = v + forcing(p, i, x, fw[x // 2, i])
                bb[p, i, pl.ds(4 * x, 4)] = v
        halo1(p).start()

    loop(NP, partial_and_send)

    for k in range(3):
        recv_b[k].wait_recv()
        send_b[4 + k].start()
    recv_a[3].wait_recv()
    send_a[7].start()
    recv_a[5].wait_recv()
    send_a[8].start()
    for k in (2, 4, 6, 7, 8):
        recv_a[k].wait_recv()
    for k in range(3, 7):
        recv_b[k].wait_recv()

    def unpack(g):
        s0[pl.ds(16 * g, 16)] = gst[g].T.reshape(16, 8, 128)

    loop(NG, unpack)


    def tables(n, now, later):
        def block(b):
            kf, dp, qm, bb_ = ([th[b, 2 * k + i] for i in range(2)] for k in range(4))
            conc = [now[i * NB + b] for i in range(2)]
            pore = [[now[(2 + 6 * i + s) * NB + b] for s in range(6)] for i in range(2)]
            cap = [qm[i] * bb_[i] for i in range(2)]
            film = [FILM * kf[i] for i in range(2)]
            for s in range(6):
                inverse = 1.0 / (1.0 + bb_[0] * pore[0][s] + bb_[1] * pore[1][s])
                u = [pore[i][s] * inverse for i in range(2)]
                for i in range(2):
                    f = 6 * i + s
                    rate = DT * cap[i] * inverse
                    kept = 1.0 - bb_[i] * u[i]
                    own = 1.0 - rate * kept
                    if s == 5:
                        own = own - film[i]
                    av[n, b, 6 * i + s] = own
                    bv[n, b, 6 * i + s] = rate * u[i] * bb_[1 - i]
                    if s == 0:
                        flux = G[0] * (pore[i][1] - pore[i][0])
                    elif s == 5:
                        flux = -(G[4] * (pore[i][5] - pore[i][4]))
                    else:
                        flux = G[s] * (pore[i][s + 1] - pore[i][s]) - G[s - 1] * (pore[i][s] - pore[i][s - 1])
                    gv[n, b, 2 + i, f] = DT * flux
                    gv[n, b, 4 + i, f] = -(DT * bb_[i]) * u[i]
                    gv[n, b, 6 + i, f] = -(DT * qm[i]) * u[i] * kept
                    gv[n, b, 7 - i, f] = rate * pore[1 - i][s] * u[i]
                    fresh = pore[i][s] + DT * dp[i] * flux - DT * cap[i] * u[i]
                    if s == 5:
                        gap = conc[i] - pore[i][5]
                        gv[n, b, i, f] = FILM * gap
                        gp[n, i, b] = -(DT * pack[b]) * gap
                        fresh = fresh + film[i] * gap
                    later[(2 + f) * NB + b] = fresh

        loop(NB, block)

    tables(0, s0, s1)

    lower = ((31, 63, 95), (127, 30, 62))
    upper = ((0, 32, 64), (96, 1, 33))

    def turned_row(r):
        return s0[192 + r // 8, pl.ds(r % 8, 1), :]

    for i in range(2):
        planes = [plane(s0[pl.ds(i * NB + 4 * x, 4)]) for x in range(3)]
        fresh = advance(
            i, planes, lambda x: s0[pl.ds((7 + 6 * i) * NB + 4 * x, 4)],
            lambda x: turned_row(lower[i][x]), lambda x: turned_row(upper[i][x]),
        )
        bs[pl.ds(4 * i, 4)] = fresh[2].reshape(4, 8, 128)
        bs[pl.ds(8 + 4 * i, 4)] = fresh[0].reshape(4, 8, 128)
        s1[pl.ds(i * NB, 4)] = fresh[0].reshape(4, 8, 128) + BEHIND * s0[pl.ds(176 + 4 * i, 4)]
        s1[pl.ds(i * NB + 4, 4)] = fresh[1].reshape(4, 8, 128)
        s1[pl.ds(i * NB + 8, 4)] = fresh[2].reshape(4, 8, 128) + AHEAD * s0[pl.ds(184 + 4 * i, 4)]
        for x in range(3):
            r = 3 * i + x
            yb1[0, NP, pl.ds(r, 1), :] = s1[i * NB + 4 * x + 3, pl.ds(7, 1), :]
            yb1[1, NP, pl.ds(r, 1), :] = s1[i * NB + 4 * x, pl.ds(0, 1), :]
    rows1(NP).start()
    turn[...] = bs[...].reshape(128, 128).T
    rsend[...] = turn[pl.ds(mine, 16), :]
    partial_state.start()
    tables(1, s1, s2)

    def whole(p):
        for i in range(2):
            c1[p, i, pl.ds(0, 4)] = bb[p, i, pl.ds(0, 4)] + BEHIND * hx0[0, p, i]
            c1[p, i, pl.ds(4, 4)] = bb[p, i, pl.ds(4, 4)] + forcing(p, i, 1, gp[0, i, pl.ds(4, 4)])
            c1[p, i, pl.ds(8, 4)] = bb[p, i, pl.ds(8, 4)] + AHEAD * hx0[1, p, i]
            for x in range(3):
                r = 3 * i + x
                yb1[0, p, pl.ds(r, 1), :] = c1[p, i, 4 * x + 3, pl.ds(7, 1), :]
                yb1[1, p, pl.ds(r, 1), :] = c1[p, i, 4 * x, pl.ds(0, 1), :]
        rows1(p).start()

    def shells(p):
        t = targ[p]
        kind, target_zone = lax.div(t, 8), lax.rem(t, 8)

        def block(b):
            within = zone[b] == target_zone
            t_now = [[sv[p, 2 + 6 * i + s, b] for s in range(6)] for i in range(2)]
            for n in range(2):
                bulk = sv if n == 0 else c1
                t_later = []
                for i in range(2):
                    flux = [ev[b, 5 * i + s] * (t_now[i][s + 1] - t_now[i][s]) for s in range(5)]
                    fresh = []
                    for s in range(6):
                        v = av[n, b, 6 * i + s] * t_now[i][s] + bv[n, b, 6 * i + s] * t_now[1 - i][s]
                        if s < 5:
                            v = v + flux[s]
                        if s > 0:
                            v = v - flux[s - 1]
                        if s == 5:
                            v = v + FILM * th[b, i] * bulk[p, i, b]
                        fresh.append(v + jnp.where(within, gv[n, b, kind, 6 * i + s], 0.0))
                    t_later.append(fresh)
                t_now = t_later
                if n == 0:
                    for i in range(2):
                        p51[p, i, b] = t_now[i][5]
            for i in range(2):
                for s in range(6):
                    out[p, 2 + 6 * i + s, b] = t_now[i][s]

        loop(NB, block)

    def step_chunk(k):
        halo0(k).wait_recv()
        for j in range(2):
            whole(2 * k + j)
        loop(2, lambda j: shells(2 * k + j))

    loop(4, step_chunk)

    from_dn = (BEHIND * AHEAD) * has_dn.astype(F32)
    from_up = (BEHIND * AHEAD) * has_up.astype(F32)

    def second(p):
        rows1(p).wait_recv()
        for i in range(2):
            planes = [plane(c1[p, i, pl.ds(4 * x, 4)]) for x in range(3)]
            fresh = advance(
                i, planes, lambda x: p51[p, i, pl.ds(4 * x, 4)],
                lambda x: yr1[0, p, pl.ds(3 * i + x, 1), :], lambda x: yr1[1, p, pl.ds(3 * i + x, 1), :],
            )
            fresh[0] = fresh[0] + from_dn * plane(sv[p, i, pl.ds(0, 4)])
            fresh[2] = fresh[2] + from_up * plane(sv[p, i, pl.ds(8, 4)])
            for x in range(3):
                out[p, i, pl.ds(4 * x, 4)] = fresh[x].reshape(4, 8, 128) + forcing(p, i, x, gp[1, i, pl.ds(4 * x, 4)])

    loop(NP, second)

    rows1(NP).wait_recv()
    for i in range(2):
        planes = [plane(s1[pl.ds(i * NB + 4 * x, 4)]) for x in range(3)]
        fresh = advance(
            i, planes, lambda x: s1[pl.ds((7 + 6 * i) * NB + 4 * x, 4)],
            lambda x: yr1[0, NP, pl.ds(3 * i + x, 1), :], lambda x: yr1[1, NP, pl.ds(3 * i + x, 1), :],
        )
        fresh[0] = fresh[0] + from_dn * plane(s0[pl.ds(i * NB, 4)])
        fresh[2] = fresh[2] + from_up * plane(s0[pl.ds(i * NB + 8, 4)])
        for x in range(3):
            s2[pl.ds(i * NB + 4 * x, 4)] = fresh[x].reshape(4, 8, 128)
    partial_state.wait_recv()
    merged = jnp.where(lane16 < 64, rrecv[0], rrecv[1])
    rolled = pltpu.roll(merged, 64, 1)
    for g in range(11):
        turn[...] = s2[pl.ds(16 * g, 16)].reshape(128, 128).T
        own = turn[pl.ds(mine, 16), :]
        if g == 0:
            own = own + jnp.where(lane16 < 32, BEHIND * merged, 0.0)
            own = own + jnp.where(lane16 >= 96, BEHIND * rolled, jnp.where(lane16 >= 64, AHEAD * merged, 0.0))
        if g == 1:
            own = own + jnp.where((lane16 >= 32) & (lane16 < 64), AHEAD * rolled, 0.0)
        for k in range(4):
            if 4 * g + k < 42:
                st_out[4 * g + k] = own[:, 32 * k : 32 * k + 32]

    def last(p):
        halo1(p).wait_recv()
        for i in range(2):
            out[p, i, pl.ds(0, 4)] = out[p, i, pl.ds(0, 4)] + BEHIND * hx1[0, p, i]
            out[p, i, pl.ds(8, 4)] = out[p, i, pl.ds(8, 4)] + AHEAD * hx1[1, p, i]

    loop(NP, last)

    halo_state.wait_send()
    partial_state.wait_send()
    rows0.wait_send()
    tile_state.wait_send()
    loop(4, lambda k: halo0(k).wait_send())
    loop(NP, lambda p: halo1(p).wait_send())
    loop(NP + 1, lambda q: rows1(q).wait_send())
    for message in send_a + send_b + send_w:
        message.wait_send()


def write_out(st, sens, st_out, out, sems):
    copies = [pltpu.make_async_copy(st, st_out, sems.at[NP])]
    copies += [pltpu.make_async_copy(sens.at[p], out.at[p], sems.at[p]) for p in range(NP)]
    for copy in copies:
        copy.start()
    for copy in copies:
        copy.wait()


def shards(state, sensitivity, packing, cell_zone, coefficients, param_target):
    packed = jnp.transpose(state, (0, 1, 3, 2)).reshape(42, 16, 32)
    vmem = pl.BlockSpec(memory_space=pltpu.VMEM)
    hbm = pl.BlockSpec(memory_space=pltpu.HBM)
    anywhere = pl.BlockSpec(memory_space=pl.ANY)
    scratch = [
        (NP, 14, NB, 8, 128),
        (NG, 128, 128), (128, 128),
        (16, 128), (2, 16, 128), (2, 2, 16, 128),
        (16, 128), (2, 16, 128), (128, 128),
        (208, 8, 128), (168, 8, 128), (176, 8, 128),
        (NB, 8, 8, 128), (NB, 10, 8, 128), (2, NB, 8, 128), (2, NB, 8, 128),
        (2, NB, 12, 8, 128), (2, NB, 12, 8, 128), (2, NB, 8, 12, 8, 128),
        (2, 2, NB, 8, 128), (2, 2, 4, 8, 128),
        (2, NP, 2, 4, 8, 128), (2, NP, 2, 4, 8, 128),
        (NP, 2, NB, 8, 128), (16, 8, 128), (NP, 2, NB, 8, 128), (NP, 2, NB, 8, 128),
        (2, NP, 8, 128), (2, NP, 8, 128), (2, NP + 1, 8, 128), (2, NP + 1, 8, 128),
        (42, 16, 32), (NB, 8, 128),
    ]
    new_state, new_sens = pl.pallas_call(
        kernel,
        out_shape=(
            jax.ShapeDtypeStruct((42, 16, 32), F32),
            jax.ShapeDtypeStruct((NP, 14, NB, 8, 128), F32),
        ),
        in_specs=[hbm] * 6,
        out_specs=(vmem, vmem),
        scratch_shapes=[pltpu.VMEM(shape, F32) for shape in scratch]
        + [
            pltpu.VMEM((NB, 8, 128), jnp.int32),
            pltpu.SMEM((8, 8), F32),
            pltpu.SMEM((NP,), jnp.int32),
            pltpu.SemaphoreType.DMA((MESSAGES,)),
            pltpu.SemaphoreType.DMA((MESSAGES,)),
            pltpu.SemaphoreType.DMA((LOCAL,)),
        ],
        compiler_params=pltpu.CompilerParams(
            collective_id=0, has_side_effects=True, vmem_limit_bytes=46 * 1024 * 1024
        ),
        name="column",
    )(
        *(
            pltpu.with_memory_space_constraint(x, pltpu.HBM)
            for x in (
                packed,
                sensitivity.reshape(NP, 14, NB, 8, 128),
                packing.reshape(NB, 8, 128),
                cell_zone.reshape(NB, 8, 128),
                coefficients,
                param_target,
            )
        )
    )
    new_state, new_sens = pl.pallas_call(
        write_out,
        out_shape=(
            jax.ShapeDtypeStruct((42, 16, 32), F32),
            jax.ShapeDtypeStruct((NP, 14, NB, 8, 128), F32),
        ),
        in_specs=[anywhere, anywhere],
        out_specs=(hbm, hbm),
        scratch_shapes=[pltpu.SemaphoreType.DMA((NP + 1,))],
        compiler_params=pltpu.CompilerParams(vmem_limit_bytes=2 * 1024 * 1024),
        name="write_out",
    )(new_state, new_sens)
    new_state = jnp.transpose(new_state.reshape(14, 3, 16, 32), (0, 1, 3, 2))
    return new_state, new_sens.reshape(NP, 14, 3, 32, 128)


def solution(mesh):
    placed = (
        P(None, "slab", "tile", "param"),
        P("param", None, "slab", "tile", None),
        P("slab", "tile", None),
        P("slab", "tile", None),
        P(),
        P("param"),
    )
    return jax.shard_map(
        shards,
        mesh=mesh,
        in_specs=placed,
        out_specs=(P(None, "slab", "tile", "param"), P("param", None, "slab", "tile", None)),
        check_vma=False,
    )
```

```python
import jax
import jax.numpy as jnp
from jax import lax
from jax.experimental import pallas as pl
from jax.experimental.pallas import tpu as pltpu
from jax.sharding import PartitionSpec as P

DT = 0.15
AHEAD = DT * 0.5
BEHIND = DT * 1.5
SIDE = DT * 0.25
CENTER = 1.0 - DT * 3.0
FILM = DT * 1.5
G = (0.3, 0.6, 0.9, 1.2, 1.5)
F32 = jnp.float32

NP = 8
NB = 12
NG = 12
ORDER = (0, 1, 7, 13, 2, 3, 4, 5, 6, 8, 9, 10, 11, 12)
SETS = ((0, 6), (6, 5))
CHUNKS = 4

X0 = 0
X1 = X0 + 2 * CHUNKS
HS = X1 + 2 * CHUNKS
RS = HS + 2
Y0 = RS + 2
Y0S = Y0 + 2
Y1 = Y0S + 2
GATHER = Y1 + 18
RELAY = GATHER + 9 * len(SETS)
DIRECT = RELAY + 6
MESSAGES = DIRECT + 7
SMALL = NP + 1
LOCAL = SMALL + 5


def at(field):
    return ORDER.index(field) * NB


def kernel(
    st_arg, sens, pack_arg, zone_arg, coef_arg, targ_arg, st_out, out,
    sv, gst, hsend, hrecv, rsend, rrecv, turn,
    s0, s1, s2, th, ev, kv, pc, av, bv, gv, gp,
    hx0, hx1, relayed, bb, bs, c1, p51, yb0, yr0, yb1, yr1,
    st_in, pack, zone, coef, targ,
    ss, rs, lsem,
):
    me, sl, ti = (lax.axis_index(a) for a in ("param", "slab", "tile"))
    h, c = lax.div(me, 2), lax.rem(me, 2)
    jp = lax.rem(h + 1, 4) * 2 + c
    jm = lax.rem(h + 3, 4) * 2 + c
    jo = lax.rem(h + 2, 4) * 2 + c
    other = 1 - 2 * c
    has_dn, has_up = sl > 0, sl < 7
    has_lo, has_hi = ti > 0, ti < 3
    up, dn = (me, sl + 1, ti), (me, sl - 1, ti)
    hi, lo = (me, sl, ti + 1), (me, sl, ti - 1)
    right, left, across, sib = (jp, sl, ti), (jm, sl, ti), (jo, sl, ti), (me + other, sl, ti)
    up2, dn2 = (me, sl + 2, ti), (me, sl - 2, ti)
    has_dn2, has_up2 = sl > 1, sl < 6
    half, odd = lax.div(sl, 2), lax.rem(sl, 2) == 1
    relay_up = jnp.where(odd & has_up, half + 1, 0)
    relay_dn = jnp.where(jnp.logical_not(odd) & has_dn, 4 - half, 0)
    relay_here = jnp.where(odd, half, jnp.maximum(3 - half, 0))

    def loop(n, body):
        lax.fori_loop(0, n, lambda i, carry: (body(i), carry)[1], 0)

    def remote(src, dst, number, device, recv_number=None):
        recv_number = number if recv_number is None else recv_number
        return pltpu.make_async_remote_copy(
            src_ref=src, dst_ref=dst, send_sem=ss.at[number], recv_sem=rs.at[recv_number],
            device_id=device, device_id_type=pl.DeviceIdType.MESH,
        )

    barrier = pltpu.get_barrier_semaphore()

    def greet(device):
        pl.semaphore_signal(barrier, inc=1, device_id=device, device_id_type=pl.DeviceIdType.MESH)

    for device in (right, left, across, sib):
        greet(device)
    others = (
        (has_up, up), (has_dn, dn), (has_hi, hi), (has_lo, lo), (has_up2, up2), (has_dn2, dn2),
    )
    for present, device in others:
        pl.when(present)(lambda device=device: greet(device))
    present_count = sum(present.astype(jnp.int32) for present, _ in others)

    bulk_copy = pltpu.make_async_copy(sens.at[:, pl.ds(0, 2)], sv.at[:, pl.ds(0, 2)], lsem.at[NP])

    def shell_copy(p):
        return pltpu.make_async_copy(
            sens.at[p, pl.ds(2, 12)], sv.at[p, pl.ds(2, 12)], lsem.at[p]
        )

    small = [
        pltpu.make_async_copy(src, dst, lsem.at[SMALL + k])
        for k, (src, dst) in enumerate(
            ((st_arg, st_in), (pack_arg, pack), (zone_arg, zone), (coef_arg, coef), (targ_arg, targ))
        )
    ]
    for copy in small:
        copy.start()
    bulk_copy.start()
    loop(NP, lambda p: shell_copy(p).start())
    pl.semaphore_wait(barrier, 4 + present_count)

    class Pair:
        def __init__(self, number, srcs, dsts, slab):
            plus, minus = (up, dn) if slab else (hi, lo)
            self.to_plus, self.to_minus = (has_up, has_dn) if slab else (has_hi, has_lo)
            self.a = remote(srcs[0], dsts[0], number, plus)
            self.b = remote(srcs[1], dsts[1], number + 1, minus)

        def start(self):
            pl.when(self.to_plus)(lambda: self.a.start())
            pl.when(self.to_minus)(lambda: self.b.start())

        def wait_recv(self):
            pl.when(self.to_minus)(lambda: self.a.wait_recv())
            pl.when(self.to_plus)(lambda: self.b.wait_recv())

        def wait_send(self):
            pl.when(self.to_plus)(lambda: self.a.wait_send())
            pl.when(self.to_minus)(lambda: self.b.wait_send())

    halo_state = Pair(HS, (hsend, hsend), (hrecv.at[0], hrecv.at[1]), True)

    class Halo:
        def __init__(self, n, k, srcs):
            base, target = ((X0, hx0), (X1, hx1))[n]
            dsts = [target.at[d, pl.ds(2 * k, 2)] for d in range(2)]
            self.direct = Pair(base + 2 * k, srcs, dsts, True)
            self.k = k
            if k < 3:
                slot, arrival = relayed.at[n, k], RELAY + 3 * n + k
                self.far = (
                    remote(srcs[0], slot, base + 2 * k, up2, arrival),
                    remote(srcs[1], slot, base + 2 * k + 1, dn2, arrival),
                )
                self.on = (
                    remote(slot, dsts[0], arrival, dn, base + 2 * k),
                    remote(slot, dsts[1], arrival, up, base + 2 * k + 1),
                )

        def start(self):
            ways = ((has_up, relay_up, self.direct.a), (has_dn, relay_dn, self.direct.b))
            for d, (present, count, copy) in enumerate(ways):
                pl.when(present & (self.k >= count))(lambda copy=copy: copy.start())
                if self.k < 3:
                    pl.when(self.k < count)(lambda d=d: self.far[d].start())

        def send_on(self):
            @pl.when(self.k < relay_here)
            def _():
                self.far[0].wait_recv()
                pl.when(odd)(lambda: self.on[0].start())
                pl.when(jnp.logical_not(odd))(lambda: self.on[1].start())

        def wait_recv(self):
            self.direct.wait_recv()

        def wait_send(self):
            self.direct.wait_send()
            if self.k < 3:
                pl.when(self.k < relay_here)(lambda: self.on[0].wait_send())

    def halo0(k):
        two, bulk = pl.ds(2 * k, 2), pl.ds(0, 2)
        return Halo(0, k, (sens.at[two, bulk, pl.ds(8, 4)], sens.at[two, bulk, pl.ds(0, 4)]))

    def halo1(k):
        two = pl.ds(2 * k, 2)
        return Halo(1, k, (bb.at[two, :, pl.ds(8, 4)], bb.at[two, :, pl.ds(0, 4)]))

    halos = [[halo0(k) for k in range(CHUNKS)], [halo1(k) for k in range(CHUNKS)]]
    partial_state = Pair(RS, (rsend, rsend), (rrecv.at[0], rrecv.at[1]), True)
    eight = pl.ds(0, NP)
    rows0 = Pair(Y0, (yb0.at[0, eight], yb0.at[1, eight]), (yr0.at[0, eight], yr0.at[1, eight]), False)

    def rows1(q):
        return Pair(Y1 + 2 * q, (yb1.at[0, q], yb1.at[1, q]), (yr1.at[0, q], yr1.at[1, q]), False)

    def shard(j, first, count):
        return gst.at[pl.ds(first, count), pl.ds(j * 16, 16)]

    rows0s = Pair(Y0S, (yb0.at[0, NP], yb0.at[1, NP]), (yr0.at[0, NP], yr0.at[1, NP]), False)

    class Gather:
        def __init__(self, first, count, number):
            def messages(shards):
                upper = count // 2
                whole, a, b = (first, count), (first, count - upper), (first + count - upper, upper)
                parts = (whole, whole, whole, a, whole, b, whole, a, b)
                devices = (right, left, sib, right, sib, left, sib, sib, sib)
                result = []
                for k in range(9):
                    ref = shard(shards[k], *parts[k])
                    result.append(remote(ref, ref, number + k, devices[k]))
                return result

            self.sent = messages((me, me, me, jm, jm, jp, jp, jo, jo))
            self.heard = messages(
                (jm, jp, me + other, jo, jm + other, jo, jp + other, jo + other, jo + other)
            )

        def start(self):
            for k in range(3):
                self.sent[k].start()

        def second(self):
            for k in range(2):
                self.heard[k].wait_recv()
                self.sent[3 + 2 * k].start()
                self.sent[4 + 2 * k].start()

        def third(self):
            for k in range(2):
                self.heard[3 + 2 * k].wait_recv()
                self.sent[7 + k].start()

        def finish(self):
            for k in (2, 4, 6, 7, 8):
                self.heard[k].wait_recv()

        def wait_send(self):
            for message in self.sent:
                message.wait_send()

    sets = [Gather(first, count, GATHER + 9 * n) for n, (first, count) in enumerate(SETS)]

    def direct_messages(shards):
        devices = (right, left, across, sib, sib, sib, sib)
        refs = [shard(j, NG - 1, 1) for j in shards]
        return [remote(ref, ref, DIRECT + k, device) for k, (ref, device) in enumerate(zip(refs, devices))]

    halo_sent = direct_messages((me, me, me, me, jm, jp, jo))
    halo_heard = direct_messages((jm, jp, jo, me + other, jm + other, jp + other, jo + other))

    small[0].wait()
    mine = pl.multiple_of(me * 16, 16)
    order = [3 * field + x for field in ORDER for x in range(3)]

    def pack_group(planes):
        blank = jnp.zeros((16, 32), F32)
        return jnp.concatenate([blank if q is None else st_in[q] for q in planes], axis=-1)

    def pack_set(n):
        for g in range(SETS[n][0], min(SETS[n][0] + SETS[n][1], 11)):
            gst[g, pl.ds(mine, 16), :] = pack_group((order + [None] * 2)[4 * g : 4 * g + 4])

    pack_set(0)
    sets[0].start()
    hsend[...] = pack_group((2, 5, 0, 3))
    halo_state.start()
    pack_set(1)
    sets[1].start()
    halos[0][0].start()

    def zero_tables(b):
        nothing = jnp.zeros((8, 128), F32)
        for n in range(2):
            for k in range(6):
                for f in range(12):
                    if k < 2 and f == 6 * k + 5 or k >= 2 and f // 6 == k % 2:
                        continue
                    gv[n, b, k, f] = nothing

    loop(NB, zero_tables)
    for copy in small[1:]:
        copy.wait()

    def clear(ref, k):
        ref[k] = jnp.zeros(ref.shape[1:], F32)

    for absent, k in ((jnp.logical_not(has_dn), 0), (jnp.logical_not(has_up), 1)):
        @pl.when(absent)
        def _(k=k):
            for ref in (hrecv, rrecv):
                clear(ref, k)
            def one(p):
                hx0[k, p] = jnp.zeros(hx0.shape[2:], F32)
                hx1[k, p] = jnp.zeros(hx1.shape[2:], F32)
            loop(NP, one)
    for absent, k in ((jnp.logical_not(has_lo), 0), (jnp.logical_not(has_hi), 1)):
        @pl.when(absent)
        def _(k=k):
            for ref in (yr0, yr1):
                clear(ref, k)

    def cell_theta(b):
        z = zone[b]
        is_zone = [z == j for j in range(1, 8)]
        values = []
        for k in range(8):
            v = jnp.full((8, 128), coef[k, 0], F32)
            for j in range(1, 8):
                v = jnp.where(is_zone[j - 1], coef[k, j], v)
            th[b, k] = v
            values.append(v)
        for i in range(2):
            exchange = DT * values[i] * pack[b]
            kv[i, b] = exchange
            pc[i, b] = CENTER - exchange
            for s in range(5):
                ev[b, 5 * i + s] = (DT * G[s]) * values[2 + i]

    loop(NB, cell_theta)

    bulk_copy.wait()

    def pack_rows0(p):
        for i in range(2):
            for x in range(3):
                r = 3 * i + x
                yb0[0, p, pl.ds(r, 1), :] = sv[p, i, 4 * x + 3, pl.ds(7, 1), :]
                yb0[1, p, pl.ds(r, 1), :] = sv[p, i, 4 * x, pl.ds(0, 1), :]

    loop(NP, pack_rows0)
    rows0.start()

    lane16 = lax.broadcasted_iota(jnp.int32, (16, 128), 1)
    halo_state.wait_recv()
    gst[NG - 1, pl.ds(mine, 16), :] = jnp.where(lane16 < 64, hrecv[0], hrecv[1])
    for k in range(4):
        halo_sent[k].start()
    sets[0].second()
    halos[0][1].start()
    sets[1].second()
    halos[0][2].start()
    halos[0][3].start()
    for k in range(3):
        halo_heard[k].wait_recv()
        halo_sent[4 + k].start()
    for gather in sets:
        gather.third()
    for gather in sets:
        gather.finish()

    def unpack(g):
        s0[pl.ds(16 * g, 16)] = gst[g].T.reshape(16, 8, 128)

    def bulk_forcing(n, state, first, count):
        for i in range(2):
            gap = state[pl.ds(i * NB + first, count)] - state[pl.ds((2 + i) * NB + first, count)]
            gp[n, i, pl.ds(first, count)] = -(DT * pack[pl.ds(first, count)]) * gap

    def state_rows(state, buffer):
        for i in range(2):
            for x in range(3):
                r = 3 * i + x
                buffer[0, NP, pl.ds(r, 1), :] = state[i * NB + 4 * x + 3, pl.ds(7, 1), :]
                buffer[1, NP, pl.ds(r, 1), :] = state[i * NB + 4 * x, pl.ds(0, 1), :]

    loop(NG - 1, unpack)
    state_rows(s0, yb0)
    rows0s.start()
    bulk_forcing(0, s0, 0, NB)
    for k in range(3):
        halos[0][k].send_on()
    row = lax.broadcasted_iota(jnp.int32, (32, 128), 0)
    lane = lax.broadcasted_iota(jnp.int32, (32, 128), 1)

    def around(v, below, above):
        return (
            jnp.where(row == 0, below, pltpu.roll(v, 1, 0))
            + jnp.where(row == 31, above, pltpu.roll(v, 31, 0))
            + jnp.where(lane == 0, 0.0, pltpu.roll(v, 1, 1))
            + jnp.where(lane == 127, 0.0, pltpu.roll(v, 127, 1))
        )

    def plane(values):
        return values.reshape(32, 128)

    def advance(i, planes, outer, below, above):
        result = []
        for x in range(3):
            four = pl.ds(4 * x, 4)
            v = planes[x]
            w = plane(pc[i, four]) * v + plane(kv[i, four]) * plane(outer(x)) + SIDE * around(v, below(x), above(x))
            if x > 0:
                w = w + BEHIND * planes[x - 1]
            if x < 2:
                w = w + AHEAD * planes[x + 1]
            result.append(w)
        return result

    def forcing(p, i, x, values):
        t = targ[p]
        target = jnp.where(lax.div(t, 8) == i, lax.rem(t, 8), -1)
        return jnp.where(zone[pl.ds(4 * x, 4)] == target, values, 0.0)

    rows0.wait_recv()

    def partial(p):
        shell_copy(p).wait()
        for i in range(2):
            planes = [plane(sv[p, i, pl.ds(4 * x, 4)]) for x in range(3)]
            fresh = advance(
                i, planes, lambda x: sv[p, 7 + 6 * i, pl.ds(4 * x, 4)],
                lambda x: yr0[0, p, pl.ds(3 * i + x, 1), :], lambda x: yr0[1, p, pl.ds(3 * i + x, 1), :],
            )
            for x in range(3):
                bb[p, i, pl.ds(4 * x, 4)] = fresh[x].reshape(4, 8, 128) + forcing(p, i, x, gp[0, i, pl.ds(4 * x, 4)])

    for k in range(3):
        loop(2, lambda j: partial(2 * k + j))
        halos[1][k].start()

    for k in range(3, 7):
        halo_heard[k].wait_recv()
    unpack(NG - 1)

    def tables(n, now, later):
        def block(b):
            kf, dp, qm, bb_ = ([th[b, 2 * k + i] for i in range(2)] for k in range(4))
            conc = [now[i * NB + b] for i in range(2)]
            pore = [[now[at(2 + 6 * i + s) + b] for s in range(6)] for i in range(2)]
            cap = [qm[i] * bb_[i] for i in range(2)]
            film = [FILM * kf[i] for i in range(2)]
            for s in range(6):
                inverse = 1.0 / (1.0 + bb_[0] * pore[0][s] + bb_[1] * pore[1][s])
                u = [pore[i][s] * inverse for i in range(2)]
                for i in range(2):
                    f = 6 * i + s
                    rate = DT * cap[i] * inverse
                    kept = 1.0 - bb_[i] * u[i]
                    own = 1.0 - rate * kept
                    if s == 5:
                        own = own - film[i]
                    av[n, b, 6 * i + s] = own
                    bv[n, b, 6 * i + s] = rate * u[i] * bb_[1 - i]
                    if s == 0:
                        flux = G[0] * (pore[i][1] - pore[i][0])
                    elif s == 5:
                        flux = -(G[4] * (pore[i][5] - pore[i][4]))
                    else:
                        flux = G[s] * (pore[i][s + 1] - pore[i][s]) - G[s - 1] * (pore[i][s] - pore[i][s - 1])
                    gv[n, b, 2 + i, f] = DT * flux
                    gv[n, b, 4 + i, f] = -(DT * bb_[i]) * u[i]
                    gv[n, b, 6 + i, f] = -(DT * qm[i]) * u[i] * kept
                    gv[n, b, 7 - i, f] = rate * pore[1 - i][s] * u[i]
                    fresh = pore[i][s] + DT * dp[i] * flux - DT * cap[i] * u[i]
                    if s == 5:
                        gap = conc[i] - pore[i][5]
                        gv[n, b, i, f] = FILM * gap
                        fresh = fresh + film[i] * gap
                    later[at(2 + f) + b] = fresh

        loop(NB, block)

    tables(0, s0, s1)

    rows0s.wait_recv()
    for i in range(2):
        planes = [plane(s0[pl.ds(i * NB + 4 * x, 4)]) for x in range(3)]
        fresh = advance(
            i, planes, lambda x: s0[pl.ds(at(7 + 6 * i) + 4 * x, 4)],
            lambda x: yr0[0, NP, pl.ds(3 * i + x, 1), :], lambda x: yr0[1, NP, pl.ds(3 * i + x, 1), :],
        )
        bs[pl.ds(4 * i, 4)] = fresh[2].reshape(4, 8, 128)
        bs[pl.ds(8 + 4 * i, 4)] = fresh[0].reshape(4, 8, 128)
        s1[pl.ds(i * NB, 4)] = fresh[0].reshape(4, 8, 128) + BEHIND * s0[pl.ds(176 + 4 * i, 4)]
        s1[pl.ds(i * NB + 4, 4)] = fresh[1].reshape(4, 8, 128)
        s1[pl.ds(i * NB + 8, 4)] = fresh[2].reshape(4, 8, 128) + AHEAD * s0[pl.ds(184 + 4 * i, 4)]
    state_rows(s1, yb1)
    rows1(NP).start()
    turn[...] = bs[...].reshape(128, 128).T
    rsend[...] = turn[pl.ds(mine, 16), :]
    partial_state.start()
    loop(2, lambda j: partial(6 + j))
    halos[1][3].start()
    halos[1][0].send_on()
    bulk_forcing(1, s1, 0, NB)
    tables(1, s1, s2)
    halos[1][1].send_on()

    def whole(p):
        for i in range(2):
            c1[p, i, pl.ds(0, 4)] = bb[p, i, pl.ds(0, 4)] + BEHIND * hx0[0, p, i]
            c1[p, i, pl.ds(4, 4)] = bb[p, i, pl.ds(4, 4)]
            c1[p, i, pl.ds(8, 4)] = bb[p, i, pl.ds(8, 4)] + AHEAD * hx0[1, p, i]
            for x in range(3):
                r = 3 * i + x
                yb1[0, p, pl.ds(r, 1), :] = c1[p, i, 4 * x + 3, pl.ds(7, 1), :]
                yb1[1, p, pl.ds(r, 1), :] = c1[p, i, 4 * x, pl.ds(0, 1), :]
        rows1(p).start()

    def shells(p):
        t = targ[p]
        kind, target_zone = lax.div(t, 8), lax.rem(t, 8)

        def block(b):
            within = zone[b] == target_zone
            t_now = [[sv[p, 2 + 6 * i + s, b] for s in range(6)] for i in range(2)]
            for n in range(2):
                bulk = sv if n == 0 else c1
                t_later = []
                for i in range(2):
                    flux = [ev[b, 5 * i + s] * (t_now[i][s + 1] - t_now[i][s]) for s in range(5)]
                    fresh = []
                    for s in range(6):
                        v = av[n, b, 6 * i + s] * t_now[i][s] + bv[n, b, 6 * i + s] * t_now[1 - i][s]
                        if s < 5:
                            v = v + flux[s]
                        if s > 0:
                            v = v - flux[s - 1]
                        if s == 5:
                            v = v + FILM * th[b, i] * bulk[p, i, b]
                        fresh.append(v + jnp.where(within, gv[n, b, kind, 6 * i + s], 0.0))
                    t_later.append(fresh)
                t_now = t_later
                if n == 0:
                    for i in range(2):
                        p51[p, i, b] = t_now[i][5]
            for i in range(2):
                for s in range(6):
                    out[p, 2 + 6 * i + s, b] = t_now[i][s]

        loop(NB, block)

    for k in range(CHUNKS):
        halos[0][k].wait_recv()
        for j in range(2):
            whole(2 * k + j)
        loop(2, lambda j: shells(2 * k + j))
        if k == 0:
            halos[1][2].send_on()

    from_dn = (BEHIND * AHEAD) * has_dn.astype(F32)
    from_up = (BEHIND * AHEAD) * has_up.astype(F32)

    def second(p):
        rows1(p).wait_recv()
        for i in range(2):
            planes = [plane(c1[p, i, pl.ds(4 * x, 4)]) for x in range(3)]
            fresh = advance(
                i, planes, lambda x: p51[p, i, pl.ds(4 * x, 4)],
                lambda x: yr1[0, p, pl.ds(3 * i + x, 1), :], lambda x: yr1[1, p, pl.ds(3 * i + x, 1), :],
            )
            fresh[0] = fresh[0] + from_dn * plane(sv[p, i, pl.ds(0, 4)])
            fresh[2] = fresh[2] + from_up * plane(sv[p, i, pl.ds(8, 4)])
            for x in range(3):
                out[p, i, pl.ds(4 * x, 4)] = fresh[x].reshape(4, 8, 128) + forcing(p, i, x, gp[1, i, pl.ds(4 * x, 4)])

    loop(NP, second)

    rows1(NP).wait_recv()
    for i in range(2):
        planes = [plane(s1[pl.ds(i * NB + 4 * x, 4)]) for x in range(3)]
        fresh = advance(
            i, planes, lambda x: s1[pl.ds(at(7 + 6 * i) + 4 * x, 4)],
            lambda x: yr1[0, NP, pl.ds(3 * i + x, 1), :], lambda x: yr1[1, NP, pl.ds(3 * i + x, 1), :],
        )
        fresh[0] = fresh[0] + from_dn * plane(s0[pl.ds(i * NB, 4)])
        fresh[2] = fresh[2] + from_up * plane(s0[pl.ds(i * NB + 8, 4)])
        for x in range(3):
            s2[pl.ds(i * NB + 4 * x, 4)] = fresh[x].reshape(4, 8, 128)
    partial_state.wait_recv()
    merged = jnp.where(lane16 < 64, rrecv[0], rrecv[1])
    rolled = pltpu.roll(merged, 64, 1)
    for g in range(11):
        turn[...] = s2[pl.ds(16 * g, 16)].reshape(128, 128).T
        own = turn[pl.ds(mine, 16), :]
        if g == 0:
            own = own + jnp.where(lane16 < 32, BEHIND * merged, 0.0)
            own = own + jnp.where(lane16 >= 96, BEHIND * rolled, jnp.where(lane16 >= 64, AHEAD * merged, 0.0))
        if g == 1:
            own = own + jnp.where((lane16 >= 32) & (lane16 < 64), AHEAD * rolled, 0.0)
        for k in range(4):
            if 4 * g + k < 42:
                st_out[order[4 * g + k]] = own[:, 32 * k : 32 * k + 32]

    def last(p):
        for i in range(2):
            out[p, i, pl.ds(0, 4)] = out[p, i, pl.ds(0, 4)] + BEHIND * hx1[0, p, i]
            out[p, i, pl.ds(8, 4)] = out[p, i, pl.ds(8, 4)] + AHEAD * hx1[1, p, i]

    for k in range(CHUNKS):
        halos[1][k].wait_recv()
        loop(2, lambda j: last(2 * k + j))

    halo_state.wait_send()
    partial_state.wait_send()
    rows0.wait_send()
    rows0s.wait_send()
    for halo in halos[0] + halos[1]:
        halo.wait_send()
    loop(NP + 1, lambda q: rows1(q).wait_send())
    for gather in sets:
        gather.wait_send()
    for message in halo_sent:
        message.wait_send()


def write_out(st, sens, st_out, out, sems):
    copies = [pltpu.make_async_copy(st, st_out, sems.at[NP])]
    copies += [pltpu.make_async_copy(sens.at[p], out.at[p], sems.at[p]) for p in range(NP)]
    for copy in copies:
        copy.start()
    for copy in copies:
        copy.wait()


def shards(state, sensitivity, packing, cell_zone, coefficients, param_target):
    packed = jnp.transpose(state, (0, 1, 3, 2)).reshape(42, 16, 32)
    vmem = pl.BlockSpec(memory_space=pltpu.VMEM)
    hbm = pl.BlockSpec(memory_space=pltpu.HBM)
    anywhere = pl.BlockSpec(memory_space=pl.ANY)
    scratch = [
        (NP, 14, NB, 8, 128),
        (NG, 128, 128),
        (16, 128), (2, 16, 128),
        (16, 128), (2, 16, 128), (128, 128),
        (192, 8, 128), (168, 8, 128), (176, 8, 128),
        (NB, 8, 8, 128), (NB, 10, 8, 128), (2, NB, 8, 128), (2, NB, 8, 128),
        (2, NB, 12, 8, 128), (2, NB, 12, 8, 128), (2, NB, 8, 12, 8, 128),
        (2, 2, NB, 8, 128),
        (2, NP, 2, 4, 8, 128), (2, NP, 2, 4, 8, 128), (2, 3, 2, 2, 4, 8, 128),
        (NP, 2, NB, 8, 128), (16, 8, 128), (NP, 2, NB, 8, 128), (NP, 2, NB, 8, 128),
        (2, NP + 1, 8, 128), (2, NP + 1, 8, 128), (2, NP + 1, 8, 128), (2, NP + 1, 8, 128),
        (42, 16, 32), (NB, 8, 128),
    ]
    new_state, new_sens = pl.pallas_call(
        kernel,
        out_shape=(
            jax.ShapeDtypeStruct((42, 16, 32), F32),
            jax.ShapeDtypeStruct((NP, 14, NB, 8, 128), F32),
        ),
        in_specs=[hbm] * 6,
        out_specs=(vmem, vmem),
        scratch_shapes=[pltpu.VMEM(shape, F32) for shape in scratch]
        + [
            pltpu.VMEM((NB, 8, 128), jnp.int32),
            pltpu.SMEM((8, 8), F32),
            pltpu.SMEM((NP,), jnp.int32),
            pltpu.SemaphoreType.DMA((MESSAGES,)),
            pltpu.SemaphoreType.DMA((MESSAGES,)),
            pltpu.SemaphoreType.DMA((LOCAL,)),
        ],
        compiler_params=pltpu.CompilerParams(
            collective_id=0, has_side_effects=True, vmem_limit_bytes=46 * 1024 * 1024
        ),
        name="column",
    )(
        *(
            pltpu.with_memory_space_constraint(x, pltpu.HBM)
            for x in (
                packed,
                sensitivity.reshape(NP, 14, NB, 8, 128),
                packing.reshape(NB, 8, 128),
                cell_zone.reshape(NB, 8, 128),
                coefficients,
                param_target,
            )
        )
    )
    new_state, new_sens = pl.pallas_call(
        write_out,
        out_shape=(
            jax.ShapeDtypeStruct((42, 16, 32), F32),
            jax.ShapeDtypeStruct((NP, 14, NB, 8, 128), F32),
        ),
        in_specs=[anywhere, anywhere],
        out_specs=(hbm, hbm),
        scratch_shapes=[pltpu.SemaphoreType.DMA((NP + 1,))],
        compiler_params=pltpu.CompilerParams(vmem_limit_bytes=2 * 1024 * 1024),
        name="write_out",
    )(new_state, new_sens)
    new_state = jnp.transpose(new_state.reshape(14, 3, 16, 32), (0, 1, 3, 2))
    return new_state, new_sens.reshape(NP, 14, 3, 32, 128)


def solution(mesh):
    placed = (
        P(None, "slab", "tile", "param"),
        P("param", None, "slab", "tile", None),
        P("slab", "tile", None),
        P("slab", "tile", None),
        P(),
        P("param"),
    )
    return jax.shard_map(
        shards,
        mesh=mesh,
        in_specs=placed,
        out_specs=(P(None, "slab", "tile", "param"), P("param", None, "slab", "tile", None)),
        check_vma=False,
    )
```

```python
import jax
import jax.numpy as jnp
from jax import lax
from jax.experimental import pallas as pl
from jax.experimental.pallas import tpu as pltpu
from jax.sharding import PartitionSpec as P

DT = 0.15
AHEAD = DT * 0.5
BEHIND = DT * 1.5
SIDE = DT * 0.25
CENTER = 1.0 - DT * 3.0
FILM = DT * 1.5
G = (0.3, 0.6, 0.9, 1.2, 1.5)
F32 = jnp.float32

NP = 8
NB = 12
NG = 12
ORDER = (0, 1, 7, 13, 2, 3, 4, 5, 6, 8, 9, 10, 11, 12)
SETS = ((0, 6), (6, 6))
CHUNKS = 8
VIA = 6

X0 = 0
X1 = X0 + 2 * CHUNKS
HS = X1 + 2 * CHUNKS
RS = HS + 2
Y0 = RS + 2
Y0S = Y0 + 2
Y1 = Y0S + 2
GATHER = Y1 + 18
RELAY = GATHER + 9 * len(SETS)
MESSAGES = RELAY + 2 * VIA
SMALL = NP + 1
LOCAL = SMALL + 5


def at(field):
    return ORDER.index(field) * NB


def kernel(
    st_arg, sens, pack_arg, zone_arg, coef_arg, targ_arg, st_out, out,
    sv, gst, hsend, hrecv, rsend, rrecv, turn,
    s0, s1, s2, th, ev, kv, pc, av, bv, gv, gp,
    hx0, hx1, relayed, bb, bs, c1, p51, yb0, yr0, yb1, yr1,
    st_in, pack, zone, coef, targ,
    ss, rs, lsem,
):
    me, sl, ti = (lax.axis_index(a) for a in ("param", "slab", "tile"))
    h, c = lax.div(me, 2), lax.rem(me, 2)
    jp = lax.rem(h + 1, 4) * 2 + c
    jm = lax.rem(h + 3, 4) * 2 + c
    jo = lax.rem(h + 2, 4) * 2 + c
    other = 1 - 2 * c
    has_dn, has_up = sl > 0, sl < 7
    has_lo, has_hi = ti > 0, ti < 3
    up, dn = (me, sl + 1, ti), (me, sl - 1, ti)
    hi, lo = (me, sl, ti + 1), (me, sl, ti - 1)
    right, left, sib = (jp, sl, ti), (jm, sl, ti), (me + other, sl, ti)
    up2, dn2 = (me, sl + 2, ti), (me, sl - 2, ti)
    has_dn2, has_up2 = sl > 1, sl < 6
    half, odd = lax.div(sl, 2), lax.rem(sl, 2) == 1
    relay_up = jnp.where(odd & has_up, 2 * half + 2, 0)
    relay_dn = jnp.where(jnp.logical_not(odd) & has_dn, 8 - 2 * half, 0)
    relay_here = jnp.where(odd, 2 * half, jnp.maximum(6 - 2 * half, 0))

    def loop(n, body):
        lax.fori_loop(0, n, lambda i, carry: (body(i), carry)[1], 0)

    def remote(src, dst, number, device, recv_number=None):
        recv_number = number if recv_number is None else recv_number
        return pltpu.make_async_remote_copy(
            src_ref=src, dst_ref=dst, send_sem=ss.at[number], recv_sem=rs.at[recv_number],
            device_id=device, device_id_type=pl.DeviceIdType.MESH,
        )

    barrier = pltpu.get_barrier_semaphore()

    def greet(device):
        pl.semaphore_signal(barrier, inc=1, device_id=device, device_id_type=pl.DeviceIdType.MESH)

    for device in (right, left, sib):
        greet(device)
    others = (
        (has_up, up), (has_dn, dn), (has_hi, hi), (has_lo, lo), (has_up2, up2), (has_dn2, dn2),
    )
    for present, device in others:
        pl.when(present)(lambda device=device: greet(device))
    present_count = sum(present.astype(jnp.int32) for present, _ in others)

    bulk_copy = pltpu.make_async_copy(sens.at[:, pl.ds(0, 2)], sv.at[:, pl.ds(0, 2)], lsem.at[NP])

    def shell_copy(p):
        return pltpu.make_async_copy(
            sens.at[p, pl.ds(2, 12)], sv.at[p, pl.ds(2, 12)], lsem.at[p]
        )

    small = [
        pltpu.make_async_copy(src, dst, lsem.at[SMALL + k])
        for k, (src, dst) in enumerate(
            ((st_arg, st_in), (pack_arg, pack), (zone_arg, zone), (coef_arg, coef), (targ_arg, targ))
        )
    ]
    for copy in small:
        copy.start()
    small[0].wait()
    mine = pl.multiple_of(me * 16, 16)
    order = [3 * field + x for field in ORDER for x in range(3)]

    def pack_group(planes):
        blank = jnp.zeros((16, 32), F32)
        return jnp.concatenate([blank if q is None else st_in[q] for q in planes], axis=-1)

    def pack_set(n):
        for g in range(SETS[n][0], min(SETS[n][0] + SETS[n][1], 11)):
            gst[g, pl.ds(mine, 16), :] = pack_group((order + [None] * 2)[4 * g : 4 * g + 4])

    pack_set(0)
    hsend[...] = pack_group((2, 5, 0, 3))

    pl.semaphore_wait(barrier, 3 + present_count)

    class Pair:
        def __init__(self, number, srcs, dsts, slab):
            plus, minus = (up, dn) if slab else (hi, lo)
            self.to_plus, self.to_minus = (has_up, has_dn) if slab else (has_hi, has_lo)
            self.a = remote(srcs[0], dsts[0], number, plus)
            self.b = remote(srcs[1], dsts[1], number + 1, minus)

        def start(self):
            pl.when(self.to_plus)(lambda: self.a.start())
            pl.when(self.to_minus)(lambda: self.b.start())

        def wait_recv(self):
            pl.when(self.to_minus)(lambda: self.a.wait_recv())
            pl.when(self.to_plus)(lambda: self.b.wait_recv())

        def wait_send(self):
            pl.when(self.to_plus)(lambda: self.a.wait_send())
            pl.when(self.to_minus)(lambda: self.b.wait_send())

    halo_state = Pair(HS, (hsend, hsend), (hrecv.at[0], hrecv.at[1]), True)

    class Halo:
        def __init__(self, n, k, srcs):
            base, target = ((X0, hx0), (X1, hx1))[n]
            dsts = [target.at[d, k] for d in range(2)]
            self.direct = Pair(base + 2 * k, srcs, dsts, True)
            self.k = k
            if k < VIA:
                slot, arrival = relayed.at[n, k], RELAY + VIA * n + k
                self.far = (
                    remote(srcs[0], slot, base + 2 * k, up2, arrival),
                    remote(srcs[1], slot, base + 2 * k + 1, dn2, arrival),
                )
                self.on = (
                    remote(slot, dsts[0], arrival, dn, base + 2 * k),
                    remote(slot, dsts[1], arrival, up, base + 2 * k + 1),
                )

        def start(self):
            ways = ((has_up, relay_up, self.direct.a), (has_dn, relay_dn, self.direct.b))
            for d, (present, count, copy) in enumerate(ways):
                pl.when(present & (self.k >= count))(lambda copy=copy: copy.start())
                if self.k < VIA:
                    pl.when(self.k < count)(lambda d=d: self.far[d].start())

        def send_on(self):
            @pl.when(self.k < relay_here)
            def _():
                self.far[0].wait_recv()
                pl.when(odd)(lambda: self.on[0].start())
                pl.when(jnp.logical_not(odd))(lambda: self.on[1].start())

        def wait_recv(self):
            self.direct.wait_recv()

        def wait_send(self):
            self.direct.wait_send()
            if self.k < VIA:
                pl.when(self.k < relay_here)(lambda: self.on[0].wait_send())

    def halo0(k):
        bulk = pl.ds(0, 2)
        return Halo(0, k, (sens.at[k, bulk, pl.ds(8, 4)], sens.at[k, bulk, pl.ds(0, 4)]))

    def halo1(k):
        return Halo(1, k, (bb.at[k, :, pl.ds(8, 4)], bb.at[k, :, pl.ds(0, 4)]))

    halos = [[halo0(k) for k in range(CHUNKS)], [halo1(k) for k in range(CHUNKS)]]
    partial_state = Pair(RS, (rsend, rsend), (rrecv.at[0], rrecv.at[1]), True)
    eight = pl.ds(0, NP)
    rows0 = Pair(Y0, (yb0.at[0, eight], yb0.at[1, eight]), (yr0.at[0, eight], yr0.at[1, eight]), False)

    def rows1(q):
        return Pair(Y1 + 2 * q, (yb1.at[0, q], yb1.at[1, q]), (yr1.at[0, q], yr1.at[1, q]), False)

    def shard(j, first, count):
        return gst.at[pl.ds(first, count), pl.ds(j * 16, 16)]

    rows0s = Pair(Y0S, (yb0.at[0, NP], yb0.at[1, NP]), (yr0.at[0, NP], yr0.at[1, NP]), False)

    class Gather:
        def __init__(self, first, count, number):
            def messages(shards):
                upper = count // 2
                whole, a, b = (first, count), (first, count - upper), (first + count - upper, upper)
                parts = (whole, whole, whole, a, whole, b, whole, a, b)
                devices = (right, left, sib, right, sib, left, sib, sib, sib)
                result = []
                for k in range(9):
                    ref = shard(shards[k], *parts[k])
                    result.append(remote(ref, ref, number + k, devices[k]))
                return result

            self.sent = messages((me, me, me, jm, jm, jp, jp, jo, jo))
            self.heard = messages(
                (jm, jp, me + other, jo, jm + other, jo, jp + other, jo + other, jo + other)
            )

        def start(self):
            for k in range(3):
                self.sent[k].start()

        def second(self):
            for k in range(2):
                self.heard[k].wait_recv()
                self.sent[3 + 2 * k].start()
                self.sent[4 + 2 * k].start()

        def third(self):
            for k in range(2):
                self.heard[3 + 2 * k].wait_recv()
                self.sent[7 + k].start()

        def finish(self):
            for k in (2, 4, 6, 7, 8):
                self.heard[k].wait_recv()

        def wait_send(self):
            for message in self.sent:
                message.wait_send()

    sets = [Gather(first, count, GATHER + 9 * n) for n, (first, count) in enumerate(SETS)]

    halo_state.start()
    sets[0].start()
    bulk_copy.start()
    loop(NP, lambda p: shell_copy(p).start())
    pack_set(1)

    def zero_tables(b):
        nothing = jnp.zeros((8, 128), F32)
        for n in range(2):
            for k in range(6):
                for f in range(12):
                    if k < 2 and f == 6 * k + 5 or k >= 2 and f // 6 == k % 2:
                        continue
                    gv[n, b, k, f] = nothing

    loop(NB, zero_tables)
    for copy in small[1:]:
        copy.wait()

    def clear(ref, k):
        ref[k] = jnp.zeros(ref.shape[1:], F32)

    for absent, k in ((jnp.logical_not(has_dn), 0), (jnp.logical_not(has_up), 1)):
        @pl.when(absent)
        def _(k=k):
            for ref in (hrecv, rrecv):
                clear(ref, k)
            def one(p):
                hx0[k, p] = jnp.zeros(hx0.shape[2:], F32)
                hx1[k, p] = jnp.zeros(hx1.shape[2:], F32)
            loop(NP, one)
    for absent, k in ((jnp.logical_not(has_lo), 0), (jnp.logical_not(has_hi), 1)):
        @pl.when(absent)
        def _(k=k):
            for ref in (yr0, yr1):
                clear(ref, k)

    def cell_theta(b):
        z = zone[b]
        is_zone = [z == j for j in range(1, 8)]
        values = []
        for k in range(8):
            v = jnp.full((8, 128), coef[k, 0], F32)
            for j in range(1, 8):
                v = jnp.where(is_zone[j - 1], coef[k, j], v)
            th[b, k] = v
            values.append(v)
        for i in range(2):
            exchange = DT * values[i] * pack[b]
            kv[i, b] = exchange
            pc[i, b] = CENTER - exchange
            for s in range(5):
                ev[b, 5 * i + s] = (DT * G[s]) * values[2 + i]

    loop(NB, cell_theta)

    bulk_copy.wait()

    def pack_rows0(p):
        for i in range(2):
            for x in range(3):
                r = 3 * i + x
                yb0[0, p, pl.ds(r, 1), :] = sv[p, i, 4 * x + 3, pl.ds(7, 1), :]
                yb0[1, p, pl.ds(r, 1), :] = sv[p, i, 4 * x, pl.ds(0, 1), :]

    loop(NP, pack_rows0)
    rows0.start()

    row = lax.broadcasted_iota(jnp.int32, (32, 128), 0)
    lane = lax.broadcasted_iota(jnp.int32, (32, 128), 1)

    def around(v, below, above):
        return (
            jnp.where(row == 0, below, pltpu.roll(v, 1, 0))
            + jnp.where(row == 31, above, pltpu.roll(v, 31, 0))
            + jnp.where(lane == 0, 0.0, pltpu.roll(v, 1, 1))
            + jnp.where(lane == 127, 0.0, pltpu.roll(v, 127, 1))
        )

    def plane(values):
        return values.reshape(32, 128)

    def advance(i, planes, outer, below, above):
        result = []
        for x in range(3):
            four = pl.ds(4 * x, 4)
            v = planes[x]
            w = plane(pc[i, four]) * v + plane(kv[i, four]) * plane(outer(x)) + SIDE * around(v, below(x), above(x))
            if x > 0:
                w = w + BEHIND * planes[x - 1]
            if x < 2:
                w = w + AHEAD * planes[x + 1]
            result.append(w)
        return result

    def forcing(p, i, values):
        t = targ[p]
        target = jnp.where(lax.div(t, 8) == i, lax.rem(t, 8), -1)
        return jnp.where(zone[...] == target, values, 0.0)

    def partial(p):
        shell_copy(p).wait()
        for i in range(2):
            planes = [plane(sv[p, i, pl.ds(4 * x, 4)]) for x in range(3)]
            fresh = advance(
                i, planes, lambda x: sv[p, 7 + 6 * i, pl.ds(4 * x, 4)],
                lambda x: yr0[0, p, pl.ds(3 * i + x, 1), :], lambda x: yr0[1, p, pl.ds(3 * i + x, 1), :],
            )
            for x in range(3):
                bb[p, i, pl.ds(4 * x, 4)] = fresh[x].reshape(4, 8, 128)

    lane16 = lax.broadcasted_iota(jnp.int32, (16, 128), 1)
    halo_state.wait_recv()
    gst[NG - 1, pl.ds(mine, 16), :] = jnp.where(lane16 < 64, hrecv[0], hrecv[1])
    sets[1].start()
    halos[0][0].start()
    sets[0].second()
    halos[0][1].start()
    sets[1].second()
    halos[0][2].start()
    halos[0][3].start()
    halos[0][4].start()
    halos[0][5].start()
    halos[0][6].start()
    halos[0][7].start()
    rows0.wait_recv()
    loop(NP, partial)
    for gather in sets:
        gather.third()
    for gather in sets:
        gather.finish()

    def unpack(g):
        s0[pl.ds(16 * g, 16)] = gst[g].T.reshape(16, 8, 128)

    def bulk_forcing(n, state, first, count):
        for i in range(2):
            gap = state[pl.ds(i * NB + first, count)] - state[pl.ds((2 + i) * NB + first, count)]
            gp[n, i, pl.ds(first, count)] = -(DT * pack[pl.ds(first, count)]) * gap

    def state_rows(state, buffer):
        for i in range(2):
            for x in range(3):
                r = 3 * i + x
                buffer[0, NP, pl.ds(r, 1), :] = state[i * NB + 4 * x + 3, pl.ds(7, 1), :]
                buffer[1, NP, pl.ds(r, 1), :] = state[i * NB + 4 * x, pl.ds(0, 1), :]

    loop(NG, unpack)
    state_rows(s0, yb0)
    rows0s.start()
    bulk_forcing(0, s0, 0, NB)
    for k in range(VIA):
        halos[0][k].send_on()
    def force(p):
        for i in range(2):
            bb[p, i] = bb[p, i] + forcing(p, i, gp[0, i])

    for k in range(6):
        force(k)
        halos[1][k].start()


    def tables(n, now, later):
        def block(b):
            kf, dp, qm, bb_ = ([th[b, 2 * k + i] for i in range(2)] for k in range(4))
            conc = [now[i * NB + b] for i in range(2)]
            pore = [[now[at(2 + 6 * i + s) + b] for s in range(6)] for i in range(2)]
            cap = [qm[i] * bb_[i] for i in range(2)]
            film = [FILM * kf[i] for i in range(2)]
            for s in range(6):
                inverse = 1.0 / (1.0 + bb_[0] * pore[0][s] + bb_[1] * pore[1][s])
                u = [pore[i][s] * inverse for i in range(2)]
                for i in range(2):
                    f = 6 * i + s
                    rate = DT * cap[i] * inverse
                    kept = 1.0 - bb_[i] * u[i]
                    own = 1.0 - rate * kept
                    if s == 5:
                        own = own - film[i]
                    av[n, b, 6 * i + s] = own
                    bv[n, b, 6 * i + s] = rate * u[i] * bb_[1 - i]
                    if s == 0:
                        flux = G[0] * (pore[i][1] - pore[i][0])
                    elif s == 5:
                        flux = -(G[4] * (pore[i][5] - pore[i][4]))
                    else:
                        flux = G[s] * (pore[i][s + 1] - pore[i][s]) - G[s - 1] * (pore[i][s] - pore[i][s - 1])
                    gv[n, b, 2 + i, f] = DT * flux
                    gv[n, b, 4 + i, f] = -(DT * bb_[i]) * u[i]
                    gv[n, b, 6 + i, f] = -(DT * qm[i]) * u[i] * kept
                    gv[n, b, 7 - i, f] = rate * pore[1 - i][s] * u[i]
                    fresh = pore[i][s] + DT * dp[i] * flux - DT * cap[i] * u[i]
                    if s == 5:
                        gap = conc[i] - pore[i][5]
                        gv[n, b, i, f] = FILM * gap
                        fresh = fresh + film[i] * gap
                    later[at(2 + f) + b] = fresh

        loop(NB, block)

    tables(0, s0, s1)

    rows0s.wait_recv()
    for i in range(2):
        planes = [plane(s0[pl.ds(i * NB + 4 * x, 4)]) for x in range(3)]
        fresh = advance(
            i, planes, lambda x: s0[pl.ds(at(7 + 6 * i) + 4 * x, 4)],
            lambda x: yr0[0, NP, pl.ds(3 * i + x, 1), :], lambda x: yr0[1, NP, pl.ds(3 * i + x, 1), :],
        )
        bs[pl.ds(4 * i, 4)] = fresh[2].reshape(4, 8, 128)
        bs[pl.ds(8 + 4 * i, 4)] = fresh[0].reshape(4, 8, 128)
        s1[pl.ds(i * NB, 4)] = fresh[0].reshape(4, 8, 128) + BEHIND * s0[pl.ds(176 + 4 * i, 4)]
        s1[pl.ds(i * NB + 4, 4)] = fresh[1].reshape(4, 8, 128)
        s1[pl.ds(i * NB + 8, 4)] = fresh[2].reshape(4, 8, 128) + AHEAD * s0[pl.ds(184 + 4 * i, 4)]
    state_rows(s1, yb1)
    rows1(NP).start()
    turn[...] = bs[...].reshape(128, 128).T
    rsend[...] = turn[pl.ds(mine, 16), :]
    partial_state.start()
    for k in range(6, CHUNKS):
        force(k)
        halos[1][k].start()
    halos[1][0].send_on()
    halos[1][1].send_on()
    bulk_forcing(1, s1, 0, NB)
    tables(1, s1, s2)
    halos[1][2].send_on()
    halos[1][3].send_on()

    def whole(p):
        for i in range(2):
            c1[p, i, pl.ds(0, 4)] = bb[p, i, pl.ds(0, 4)] + BEHIND * hx0[0, p, i]
            c1[p, i, pl.ds(4, 4)] = bb[p, i, pl.ds(4, 4)]
            c1[p, i, pl.ds(8, 4)] = bb[p, i, pl.ds(8, 4)] + AHEAD * hx0[1, p, i]
            for x in range(3):
                r = 3 * i + x
                yb1[0, p, pl.ds(r, 1), :] = c1[p, i, 4 * x + 3, pl.ds(7, 1), :]
                yb1[1, p, pl.ds(r, 1), :] = c1[p, i, 4 * x, pl.ds(0, 1), :]
        rows1(p).start()

    def shells(p):
        t = targ[p]
        kind, target_zone = lax.div(t, 8), lax.rem(t, 8)

        def block(b):
            within = zone[b] == target_zone
            t_now = [[sv[p, 2 + 6 * i + s, b] for s in range(6)] for i in range(2)]
            for n in range(2):
                bulk = sv if n == 0 else c1
                t_later = []
                for i in range(2):
                    flux = [ev[b, 5 * i + s] * (t_now[i][s + 1] - t_now[i][s]) for s in range(5)]
                    fresh = []
                    for s in range(6):
                        v = av[n, b, 6 * i + s] * t_now[i][s] + bv[n, b, 6 * i + s] * t_now[1 - i][s]
                        if s < 5:
                            v = v + flux[s]
                        if s > 0:
                            v = v - flux[s - 1]
                        if s == 5:
                            v = v + FILM * th[b, i] * bulk[p, i, b]
                        fresh.append(v + jnp.where(within, gv[n, b, kind, 6 * i + s], 0.0))
                    t_later.append(fresh)
                t_now = t_later
                if n == 0:
                    for i in range(2):
                        p51[p, i, b] = t_now[i][5]
            for i in range(2):
                for s in range(6):
                    out[p, 2 + 6 * i + s, b] = t_now[i][s]

        loop(NB, block)

    for k in range(4):
        for j in range(2):
            halos[0][2 * k + j].wait_recv()
            whole(2 * k + j)
        loop(2, lambda j: shells(2 * k + j))
        if k < 2:
            halos[1][4 + k].send_on()

    from_dn = (BEHIND * AHEAD) * has_dn.astype(F32)
    from_up = (BEHIND * AHEAD) * has_up.astype(F32)

    def second(p):
        rows1(p).wait_recv()
        for i in range(2):
            planes = [plane(c1[p, i, pl.ds(4 * x, 4)]) for x in range(3)]
            fresh = advance(
                i, planes, lambda x: p51[p, i, pl.ds(4 * x, 4)],
                lambda x: yr1[0, p, pl.ds(3 * i + x, 1), :], lambda x: yr1[1, p, pl.ds(3 * i + x, 1), :],
            )
            fresh[0] = fresh[0] + from_dn * plane(sv[p, i, pl.ds(0, 4)])
            fresh[2] = fresh[2] + from_up * plane(sv[p, i, pl.ds(8, 4)])
            force_now = forcing(p, i, gp[1, i])
            for x in range(3):
                out[p, i, pl.ds(4 * x, 4)] = fresh[x].reshape(4, 8, 128) + force_now[4 * x : 4 * x + 4]

    loop(NP, second)

    rows1(NP).wait_recv()
    for i in range(2):
        planes = [plane(s1[pl.ds(i * NB + 4 * x, 4)]) for x in range(3)]
        fresh = advance(
            i, planes, lambda x: s1[pl.ds(at(7 + 6 * i) + 4 * x, 4)],
            lambda x: yr1[0, NP, pl.ds(3 * i + x, 1), :], lambda x: yr1[1, NP, pl.ds(3 * i + x, 1), :],
        )
        fresh[0] = fresh[0] + from_dn * plane(s0[pl.ds(i * NB, 4)])
        fresh[2] = fresh[2] + from_up * plane(s0[pl.ds(i * NB + 8, 4)])
        for x in range(3):
            s2[pl.ds(i * NB + 4 * x, 4)] = fresh[x].reshape(4, 8, 128)
    partial_state.wait_recv()
    merged = jnp.where(lane16 < 64, rrecv[0], rrecv[1])
    rolled = pltpu.roll(merged, 64, 1)
    for g in range(11):
        turn[...] = s2[pl.ds(16 * g, 16)].reshape(128, 128).T
        own = turn[pl.ds(mine, 16), :]
        if g == 0:
            own = own + jnp.where(lane16 < 32, BEHIND * merged, 0.0)
            own = own + jnp.where(lane16 >= 96, BEHIND * rolled, jnp.where(lane16 >= 64, AHEAD * merged, 0.0))
        if g == 1:
            own = own + jnp.where((lane16 >= 32) & (lane16 < 64), AHEAD * rolled, 0.0)
        for k in range(4):
            if 4 * g + k < 42:
                st_out[order[4 * g + k]] = own[:, 32 * k : 32 * k + 32]

    def last(p):
        for i in range(2):
            out[p, i, pl.ds(0, 4)] = out[p, i, pl.ds(0, 4)] + BEHIND * hx1[0, p, i]
            out[p, i, pl.ds(8, 4)] = out[p, i, pl.ds(8, 4)] + AHEAD * hx1[1, p, i]

    for k in range(CHUNKS):
        halos[1][k].wait_recv()
        last(k)

    halo_state.wait_send()
    partial_state.wait_send()
    rows0.wait_send()
    rows0s.wait_send()
    for halo in halos[0] + halos[1]:
        halo.wait_send()
    loop(NP + 1, lambda q: rows1(q).wait_send())
    for gather in sets:
        gather.wait_send()


def write_out(st, sens, st_out, out, sems):
    copies = [pltpu.make_async_copy(st, st_out, sems.at[NP])]
    copies += [pltpu.make_async_copy(sens.at[p], out.at[p], sems.at[p]) for p in range(NP)]
    for copy in copies:
        copy.start()
    for copy in copies:
        copy.wait()


def shards(state, sensitivity, packing, cell_zone, coefficients, param_target):
    packed = jnp.transpose(state, (0, 1, 3, 2)).reshape(42, 16, 32)
    vmem = pl.BlockSpec(memory_space=pltpu.VMEM)
    hbm = pl.BlockSpec(memory_space=pltpu.HBM)
    anywhere = pl.BlockSpec(memory_space=pl.ANY)
    scratch = [
        (NP, 14, NB, 8, 128),
        (NG, 128, 128),
        (16, 128), (2, 16, 128),
        (16, 128), (2, 16, 128), (128, 128),
        (192, 8, 128), (168, 8, 128), (176, 8, 128),
        (NB, 8, 8, 128), (NB, 10, 8, 128), (2, NB, 8, 128), (2, NB, 8, 128),
        (2, NB, 12, 8, 128), (2, NB, 12, 8, 128), (2, NB, 8, 12, 8, 128),
        (2, 2, NB, 8, 128),
        (2, NP, 2, 4, 8, 128), (2, NP, 2, 4, 8, 128), (2, VIA, 2, 4, 8, 128),
        (NP, 2, NB, 8, 128), (16, 8, 128), (NP, 2, NB, 8, 128), (NP, 2, NB, 8, 128),
        (2, NP + 1, 8, 128), (2, NP + 1, 8, 128), (2, NP + 1, 8, 128), (2, NP + 1, 8, 128),
        (42, 16, 32), (NB, 8, 128),
    ]
    new_state, new_sens = pl.pallas_call(
        kernel,
        out_shape=(
            jax.ShapeDtypeStruct((42, 16, 32), F32),
            jax.ShapeDtypeStruct((NP, 14, NB, 8, 128), F32),
        ),
        in_specs=[hbm] * 6,
        out_specs=(vmem, vmem),
        scratch_shapes=[pltpu.VMEM(shape, F32) for shape in scratch]
        + [
            pltpu.VMEM((NB, 8, 128), jnp.int32),
            pltpu.SMEM((8, 8), F32),
            pltpu.SMEM((NP,), jnp.int32),
            pltpu.SemaphoreType.DMA((MESSAGES,)),
            pltpu.SemaphoreType.DMA((MESSAGES,)),
            pltpu.SemaphoreType.DMA((LOCAL,)),
        ],
        compiler_params=pltpu.CompilerParams(
            collective_id=0, has_side_effects=True, vmem_limit_bytes=46 * 1024 * 1024
        ),
        name="column",
    )(
        *(
            pltpu.with_memory_space_constraint(x, pltpu.HBM)
            for x in (
                packed,
                sensitivity.reshape(NP, 14, NB, 8, 128),
                packing.reshape(NB, 8, 128),
                cell_zone.reshape(NB, 8, 128),
                coefficients,
                param_target,
            )
        )
    )
    new_state, new_sens = pl.pallas_call(
        write_out,
        out_shape=(
            jax.ShapeDtypeStruct((42, 16, 32), F32),
            jax.ShapeDtypeStruct((NP, 14, NB, 8, 128), F32),
        ),
        in_specs=[anywhere, anywhere],
        out_specs=(hbm, hbm),
        scratch_shapes=[pltpu.SemaphoreType.DMA((NP + 1,))],
        compiler_params=pltpu.CompilerParams(vmem_limit_bytes=2 * 1024 * 1024),
        name="write_out",
    )(new_state, new_sens)
    new_state = jnp.transpose(new_state.reshape(14, 3, 16, 32), (0, 1, 3, 2))
    return new_state, new_sens.reshape(NP, 14, 3, 32, 128)


def solution(mesh):
    placed = (
        P(None, "slab", "tile", "param"),
        P("param", None, "slab", "tile", None),
        P("slab", "tile", None),
        P("slab", "tile", None),
        P(),
        P("param"),
    )
    return jax.shard_map(
        shards,
        mesh=mesh,
        in_specs=placed,
        out_specs=(P(None, "slab", "tile", "param"), P("param", None, "slab", "tile", None)),
        check_vma=False,
    )
```

```python
import jax
import jax.numpy as jnp
from jax import lax
from jax.experimental import pallas as pl
from jax.experimental.pallas import tpu as pltpu
from jax.sharding import PartitionSpec as P

DT = 0.15
AHEAD = DT * 0.5
BEHIND = DT * 1.5
SIDE = DT * 0.25
CENTER = 1.0 - DT * 3.0
FILM = DT * 1.5
G = (0.3, 0.6, 0.9, 1.2, 1.5)
F32 = jnp.float32

NP = 8
NB = 12
NG = 12
ORDER = (0, 1, 7, 13, 2, 3, 4, 5, 6, 8, 9, 10, 11, 12)
SETS = ((0, 6), (6, 6))
CHUNKS = 8
VIA = 6

X0 = 0
X1 = X0 + 2 * CHUNKS
HS = X1 + 2 * CHUNKS
RS = HS + 2
Y0 = RS + 2
Y0S = Y0 + 2
Y1 = Y0S + 2
GATHER = Y1 + 18
RELAY = GATHER + 9 * len(SETS)
MESSAGES = RELAY + 2 * VIA
SMALL = NP + 1
LOCAL = SMALL + 5


def at(field):
    return ORDER.index(field) * NB


def kernel(
    st_arg, sens, pack_arg, zone_arg, coef_arg, targ_arg, st_out, out,
    sv, gst, hsend, hrecv, rsend, rrecv, turn,
    s0, s1, s2, th, ev, kv, pc, av, bv, gv, gp,
    hx0, hx1, relayed, bb, bs, c1, p51, yb0, yr0, yb1, yr1,
    st_in, pack, zone, coef, targ,
    ss, rs, lsem,
):
    me, sl, ti = (lax.axis_index(a) for a in ("param", "slab", "tile"))
    h, c = lax.div(me, 2), lax.rem(me, 2)
    jp = lax.rem(h + 1, 4) * 2 + c
    jm = lax.rem(h + 3, 4) * 2 + c
    jo = lax.rem(h + 2, 4) * 2 + c
    other = 1 - 2 * c
    has_dn, has_up = sl > 0, sl < 7
    has_lo, has_hi = ti > 0, ti < 3
    up, dn = (me, sl + 1, ti), (me, sl - 1, ti)
    hi, lo = (me, sl, ti + 1), (me, sl, ti - 1)
    right, left, sib = (jp, sl, ti), (jm, sl, ti), (me + other, sl, ti)
    up2, dn2 = (me, sl + 2, ti), (me, sl - 2, ti)
    has_dn2, has_up2 = sl > 1, sl < 6
    half, odd = lax.div(sl, 2), lax.rem(sl, 2) == 1
    relay_up = jnp.where(odd & has_up, 2 * half + 2, 0)
    relay_dn = jnp.where(jnp.logical_not(odd) & has_dn, 8 - 2 * half, 0)
    relay_here = jnp.where(odd, 2 * half, jnp.maximum(6 - 2 * half, 0))

    def loop(n, body):
        lax.fori_loop(0, n, lambda i, carry: (body(i), carry)[1], 0)

    def remote(src, dst, number, device, recv_number=None):
        recv_number = number if recv_number is None else recv_number
        return pltpu.make_async_remote_copy(
            src_ref=src, dst_ref=dst, send_sem=ss.at[number], recv_sem=rs.at[recv_number],
            device_id=device, device_id_type=pl.DeviceIdType.MESH,
        )

    barrier = pltpu.get_barrier_semaphore()

    def greet(device):
        pl.semaphore_signal(barrier, inc=1, device_id=device, device_id_type=pl.DeviceIdType.MESH)

    for device in (right, left, sib):
        greet(device)
    others = (
        (has_up, up), (has_dn, dn), (has_hi, hi), (has_lo, lo), (has_up2, up2), (has_dn2, dn2),
    )
    for present, device in others:
        pl.when(present)(lambda device=device: greet(device))
    present_count = sum(present.astype(jnp.int32) for present, _ in others)

    bulk_copy = pltpu.make_async_copy(sens.at[:, pl.ds(0, 2)], sv.at[:, pl.ds(0, 2)], lsem.at[NP])

    def shell_copy(p):
        return pltpu.make_async_copy(
            sens.at[p, pl.ds(2, 12)], sv.at[p, pl.ds(2, 12)], lsem.at[p]
        )

    small = [
        pltpu.make_async_copy(src, dst, lsem.at[SMALL + k])
        for k, (src, dst) in enumerate(
            ((st_arg, st_in), (pack_arg, pack), (zone_arg, zone), (coef_arg, coef), (targ_arg, targ))
        )
    ]
    for copy in small:
        copy.start()
    small[0].wait()
    mine = pl.multiple_of(me * 16, 16)
    order = [3 * field + x for field in ORDER for x in range(3)]

    def pack_group(planes):
        blank = jnp.zeros((16, 32), F32)
        return jnp.concatenate([blank if q is None else st_in[q] for q in planes], axis=-1)

    def pack_set(n):
        for g in range(SETS[n][0], min(SETS[n][0] + SETS[n][1], 11)):
            gst[g, pl.ds(mine, 16), :] = pack_group((order + [None] * 2)[4 * g : 4 * g + 4])

    pack_set(0)
    hsend[...] = pack_group((2, 5, 0, 3))

    pl.semaphore_wait(barrier, 3 + present_count)

    class Pair:
        def __init__(self, number, srcs, dsts, slab):
            plus, minus = (up, dn) if slab else (hi, lo)
            self.to_plus, self.to_minus = (has_up, has_dn) if slab else (has_hi, has_lo)
            self.a = remote(srcs[0], dsts[0], number, plus)
            self.b = remote(srcs[1], dsts[1], number + 1, minus)

        def start(self):
            pl.when(self.to_plus)(lambda: self.a.start())
            pl.when(self.to_minus)(lambda: self.b.start())

        def wait_recv(self):
            pl.when(self.to_minus)(lambda: self.a.wait_recv())
            pl.when(self.to_plus)(lambda: self.b.wait_recv())

        def wait_send(self):
            pl.when(self.to_plus)(lambda: self.a.wait_send())
            pl.when(self.to_minus)(lambda: self.b.wait_send())

    halo_state = Pair(HS, (hsend, hsend), (hrecv.at[0], hrecv.at[1]), True)

    class Halo:
        def __init__(self, n, k, srcs):
            base, target = ((X0, hx0), (X1, hx1))[n]
            dsts = [target.at[d, k] for d in range(2)]
            self.direct = Pair(base + 2 * k, srcs, dsts, True)
            self.k = k
            if k < VIA:
                slot, arrival = relayed.at[n, k], RELAY + VIA * n + k
                self.far = (
                    remote(srcs[0], slot, base + 2 * k, up2, arrival),
                    remote(srcs[1], slot, base + 2 * k + 1, dn2, arrival),
                )
                self.on = (
                    remote(slot, dsts[0], arrival, dn, base + 2 * k),
                    remote(slot, dsts[1], arrival, up, base + 2 * k + 1),
                )

        def start(self):
            ways = ((has_up, relay_up, self.direct.a), (has_dn, relay_dn, self.direct.b))
            for d, (present, count, copy) in enumerate(ways):
                pl.when(present & (self.k >= count))(lambda copy=copy: copy.start())
                if self.k < VIA:
                    pl.when(self.k < count)(lambda d=d: self.far[d].start())

        def send_on(self):
            @pl.when(self.k < relay_here)
            def _():
                self.far[0].wait_recv()
                pl.when(odd)(lambda: self.on[0].start())
                pl.when(jnp.logical_not(odd))(lambda: self.on[1].start())

        def wait_recv(self):
            self.direct.wait_recv()

        def wait_send(self):
            self.direct.wait_send()
            if self.k < VIA:
                pl.when(self.k < relay_here)(lambda: self.on[0].wait_send())

    def halo0(k):
        bulk = pl.ds(0, 2)
        return Halo(0, k, (sens.at[k, bulk, pl.ds(8, 4)], sens.at[k, bulk, pl.ds(0, 4)]))

    def halo1(k):
        return Halo(1, k, (bb.at[k, :, pl.ds(8, 4)], bb.at[k, :, pl.ds(0, 4)]))

    halos = [[halo0(k) for k in range(CHUNKS)], [halo1(k) for k in range(CHUNKS)]]
    partial_state = Pair(RS, (rsend, rsend), (rrecv.at[0], rrecv.at[1]), True)
    eight = pl.ds(0, NP)
    rows0 = Pair(Y0, (yb0.at[0, eight], yb0.at[1, eight]), (yr0.at[0, eight], yr0.at[1, eight]), False)

    def rows1(q):
        return Pair(Y1 + 2 * q, (yb1.at[0, q], yb1.at[1, q]), (yr1.at[0, q], yr1.at[1, q]), False)

    def shard(j, first, count):
        return gst.at[pl.ds(first, count), pl.ds(j * 16, 16)]

    rows0s = Pair(Y0S, (yb0.at[0, NP], yb0.at[1, NP]), (yr0.at[0, NP], yr0.at[1, NP]), False)

    class Gather:
        def __init__(self, first, count, number):
            def messages(shards):
                upper = count // 2
                whole, a, b = (first, count), (first, count - upper), (first + count - upper, upper)
                parts = (whole, whole, whole, a, whole, b, whole, a, b)
                devices = (right, left, sib, right, sib, left, sib, sib, sib)
                result = []
                for k in range(9):
                    ref = shard(shards[k], *parts[k])
                    result.append(remote(ref, ref, number + k, devices[k]))
                return result

            self.sent = messages((me, me, me, jm, jm, jp, jp, jo, jo))
            self.heard = messages(
                (jm, jp, me + other, jo, jm + other, jo, jp + other, jo + other, jo + other)
            )

        def start(self):
            for k in range(3):
                self.sent[k].start()

        def second(self):
            for k in range(2):
                self.heard[k].wait_recv()
                self.sent[3 + 2 * k].start()
                self.sent[4 + 2 * k].start()

        def third(self):
            for k in range(2):
                self.heard[3 + 2 * k].wait_recv()
                self.sent[7 + k].start()

        def finish(self):
            for k in (2, 4, 6, 7, 8):
                self.heard[k].wait_recv()

        def wait_send(self):
            for message in self.sent:
                message.wait_send()

    sets = [Gather(first, count, GATHER + 9 * n) for n, (first, count) in enumerate(SETS)]

    halo_state.start()
    sets[0].start()
    bulk_copy.start()
    loop(NP, lambda p: shell_copy(p).start())
    pack_set(1)

    def zero_tables(b):
        nothing = jnp.zeros((8, 128), F32)
        for n in range(2):
            for k in range(6):
                for f in range(12):
                    if k < 2 and f == 6 * k + 5 or k >= 2 and f // 6 == k % 2:
                        continue
                    gv[n, b, k, f] = nothing

    loop(NB, zero_tables)
    for copy in small[1:]:
        copy.wait()

    def clear(ref, k):
        ref[k] = jnp.zeros(ref.shape[1:], F32)

    for absent, k in ((jnp.logical_not(has_dn), 0), (jnp.logical_not(has_up), 1)):
        @pl.when(absent)
        def _(k=k):
            for ref in (hrecv, rrecv):
                clear(ref, k)
            def one(p):
                hx0[k, p] = jnp.zeros(hx0.shape[2:], F32)
                hx1[k, p] = jnp.zeros(hx1.shape[2:], F32)
            loop(NP, one)
    for absent, k in ((jnp.logical_not(has_lo), 0), (jnp.logical_not(has_hi), 1)):
        @pl.when(absent)
        def _(k=k):
            for ref in (yr0, yr1):
                clear(ref, k)

    def cell_theta(b):
        z = zone[b]
        is_zone = [z == j for j in range(1, 8)]
        values = []
        for k in range(8):
            v = jnp.full((8, 128), coef[k, 0], F32)
            for j in range(1, 8):
                v = jnp.where(is_zone[j - 1], coef[k, j], v)
            th[b, k] = v
            values.append(v)
        for i in range(2):
            exchange = DT * values[i] * pack[b]
            kv[i, b] = exchange
            pc[i, b] = CENTER - exchange
            for s in range(5):
                ev[b, 5 * i + s] = (DT * G[s]) * values[2 + i]

    loop(NB, cell_theta)

    bulk_copy.wait()

    def pack_rows0(p):
        for i in range(2):
            for x in range(3):
                r = 3 * i + x
                yb0[0, p, pl.ds(r, 1), :] = sv[p, i, 4 * x + 3, pl.ds(7, 1), :]
                yb0[1, p, pl.ds(r, 1), :] = sv[p, i, 4 * x, pl.ds(0, 1), :]

    loop(NP, pack_rows0)
    rows0.start()

    row = lax.broadcasted_iota(jnp.int32, (32, 128), 0)
    lane = lax.broadcasted_iota(jnp.int32, (32, 128), 1)

    def around(v, below, above):
        return (
            jnp.where(row == 0, below, pltpu.roll(v, 1, 0))
            + jnp.where(row == 31, above, pltpu.roll(v, 31, 0))
            + jnp.where(lane == 0, 0.0, pltpu.roll(v, 1, 1))
            + jnp.where(lane == 127, 0.0, pltpu.roll(v, 127, 1))
        )

    def plane(values):
        return values.reshape(32, 128)

    def advance(i, planes, outer, below, above):
        result = []
        for x in range(3):
            four = pl.ds(4 * x, 4)
            v = planes[x]
            w = plane(pc[i, four]) * v + plane(kv[i, four]) * plane(outer(x)) + SIDE * around(v, below(x), above(x))
            if x > 0:
                w = w + BEHIND * planes[x - 1]
            if x < 2:
                w = w + AHEAD * planes[x + 1]
            result.append(w)
        return result

    def forcing(p, i, values):
        t = targ[p]
        target = jnp.where(lax.div(t, 8) == i, lax.rem(t, 8), -1)
        return jnp.where(zone[...] == target, values, 0.0)

    def partial(p):
        shell_copy(p).wait()
        for i in range(2):
            planes = [plane(sv[p, i, pl.ds(4 * x, 4)]) for x in range(3)]
            fresh = advance(
                i, planes, lambda x: sv[p, 7 + 6 * i, pl.ds(4 * x, 4)],
                lambda x: yr0[0, p, pl.ds(3 * i + x, 1), :], lambda x: yr0[1, p, pl.ds(3 * i + x, 1), :],
            )
            for x in range(3):
                bb[p, i, pl.ds(4 * x, 4)] = fresh[x].reshape(4, 8, 128)

    lane16 = lax.broadcasted_iota(jnp.int32, (16, 128), 1)
    halo_state.wait_recv()
    gst[NG - 1, pl.ds(mine, 16), :] = jnp.where(lane16 < 64, hrecv[0], hrecv[1])
    sets[1].start()
    halos[0][0].start()
    sets[0].second()
    halos[0][1].start()
    sets[1].second()
    halos[0][2].start()
    halos[0][3].start()
    halos[0][4].start()
    halos[0][5].start()
    halos[0][6].start()
    halos[0][7].start()
    rows0.wait_recv()
    loop(NP, partial)
    for gather in sets:
        gather.third()
    for gather in sets:
        gather.finish()

    def unpack(g):
        s0[pl.ds(16 * g, 16)] = gst[g].T.reshape(16, 8, 128)

    def bulk_forcing(n, state, first, count):
        for i in range(2):
            gap = state[pl.ds(i * NB + first, count)] - state[pl.ds((2 + i) * NB + first, count)]
            gp[n, i, pl.ds(first, count)] = -(DT * pack[pl.ds(first, count)]) * gap

    def state_rows(state, buffer):
        for i in range(2):
            for x in range(3):
                r = 3 * i + x
                buffer[0, NP, pl.ds(r, 1), :] = state[i * NB + 4 * x + 3, pl.ds(7, 1), :]
                buffer[1, NP, pl.ds(r, 1), :] = state[i * NB + 4 * x, pl.ds(0, 1), :]

    loop(NG, unpack)
    state_rows(s0, yb0)
    rows0s.start()
    bulk_forcing(0, s0, 0, NB)
    for k in range(VIA):
        halos[0][k].send_on()
    def force(p):
        for i in range(2):
            bb[p, i] = bb[p, i] + forcing(p, i, gp[0, i])

    for k in range(6):
        force(k)
        halos[1][k].start()


    def tables(n, now, later):
        def block(b):
            kf, dp, qm, bb_ = ([th[b, 2 * k + i] for i in range(2)] for k in range(4))
            conc = [now[i * NB + b] for i in range(2)]
            pore = [[now[at(2 + 6 * i + s) + b] for s in range(6)] for i in range(2)]
            cap = [qm[i] * bb_[i] for i in range(2)]
            film = [FILM * kf[i] for i in range(2)]
            for s in range(6):
                inverse = 1.0 / (1.0 + bb_[0] * pore[0][s] + bb_[1] * pore[1][s])
                u = [pore[i][s] * inverse for i in range(2)]
                for i in range(2):
                    f = 6 * i + s
                    rate = DT * cap[i] * inverse
                    kept = 1.0 - bb_[i] * u[i]
                    own = 1.0 - rate * kept
                    if s == 5:
                        own = own - film[i]
                    av[n, b, 6 * i + s] = own
                    bv[n, b, 6 * i + s] = rate * u[i] * bb_[1 - i]
                    if s == 0:
                        flux = G[0] * (pore[i][1] - pore[i][0])
                    elif s == 5:
                        flux = -(G[4] * (pore[i][5] - pore[i][4]))
                    else:
                        flux = G[s] * (pore[i][s + 1] - pore[i][s]) - G[s - 1] * (pore[i][s] - pore[i][s - 1])
                    gv[n, b, 2 + i, f] = DT * flux
                    gv[n, b, 4 + i, f] = -(DT * bb_[i]) * u[i]
                    gv[n, b, 6 + i, f] = -(DT * qm[i]) * u[i] * kept
                    gv[n, b, 7 - i, f] = rate * pore[1 - i][s] * u[i]
                    fresh = pore[i][s] + DT * dp[i] * flux - DT * cap[i] * u[i]
                    if s == 5:
                        gap = conc[i] - pore[i][5]
                        gv[n, b, i, f] = FILM * gap
                        fresh = fresh + film[i] * gap
                    later[at(2 + f) + b] = fresh

        loop(NB, block)

    tables(0, s0, s1)

    rows0s.wait_recv()
    for i in range(2):
        planes = [plane(s0[pl.ds(i * NB + 4 * x, 4)]) for x in range(3)]
        fresh = advance(
            i, planes, lambda x: s0[pl.ds(at(7 + 6 * i) + 4 * x, 4)],
            lambda x: yr0[0, NP, pl.ds(3 * i + x, 1), :], lambda x: yr0[1, NP, pl.ds(3 * i + x, 1), :],
        )
        bs[pl.ds(4 * i, 4)] = fresh[2].reshape(4, 8, 128)
        bs[pl.ds(8 + 4 * i, 4)] = fresh[0].reshape(4, 8, 128)
        s1[pl.ds(i * NB, 4)] = fresh[0].reshape(4, 8, 128) + BEHIND * s0[pl.ds(176 + 4 * i, 4)]
        s1[pl.ds(i * NB + 4, 4)] = fresh[1].reshape(4, 8, 128)
        s1[pl.ds(i * NB + 8, 4)] = fresh[2].reshape(4, 8, 128) + AHEAD * s0[pl.ds(184 + 4 * i, 4)]
    state_rows(s1, yb1)
    rows1(NP).start()
    turn[...] = bs[...].reshape(128, 128).T
    rsend[...] = turn[pl.ds(mine, 16), :]
    partial_state.start()
    for k in range(6, CHUNKS):
        force(k)
        halos[1][k].start()
    halos[1][0].send_on()
    halos[1][1].send_on()
    bulk_forcing(1, s1, 0, NB)
    tables(1, s1, s2)
    halos[1][2].send_on()
    halos[1][3].send_on()

    def whole(p):
        for i in range(2):
            c1[p, i, pl.ds(0, 4)] = bb[p, i, pl.ds(0, 4)] + BEHIND * hx0[0, p, i]
            c1[p, i, pl.ds(4, 4)] = bb[p, i, pl.ds(4, 4)]
            c1[p, i, pl.ds(8, 4)] = bb[p, i, pl.ds(8, 4)] + AHEAD * hx0[1, p, i]
            for x in range(3):
                r = 3 * i + x
                yb1[0, p, pl.ds(r, 1), :] = c1[p, i, 4 * x + 3, pl.ds(7, 1), :]
                yb1[1, p, pl.ds(r, 1), :] = c1[p, i, 4 * x, pl.ds(0, 1), :]
        rows1(p).start()

    def shells(p):
        t = targ[p]
        kind, target_zone = lax.div(t, 8), lax.rem(t, 8)

        def block(b):
            within = zone[b] == target_zone
            t_now = [[sv[p, 2 + 6 * i + s, b] for s in range(6)] for i in range(2)]
            for n in range(2):
                bulk = sv if n == 0 else c1
                t_later = []
                for i in range(2):
                    flux = [ev[b, 5 * i + s] * (t_now[i][s + 1] - t_now[i][s]) for s in range(5)]
                    fresh = []
                    for s in range(6):
                        v = av[n, b, 6 * i + s] * t_now[i][s] + bv[n, b, 6 * i + s] * t_now[1 - i][s]
                        if s < 5:
                            v = v + flux[s]
                        if s > 0:
                            v = v - flux[s - 1]
                        if s == 5:
                            v = v + FILM * th[b, i] * bulk[p, i, b]
                        fresh.append(v + jnp.where(within, gv[n, b, kind, 6 * i + s], 0.0))
                    t_later.append(fresh)
                t_now = t_later
                if n == 0:
                    for i in range(2):
                        p51[p, i, b] = t_now[i][5]
            for i in range(2):
                for s in range(6):
                    out[p, 2 + 6 * i + s, b] = t_now[i][s]

        loop(NB, block)

    for k in range(4):
        for j in range(2):
            halos[0][2 * k + j].wait_recv()
            whole(2 * k + j)
        loop(2, lambda j: shells(2 * k + j))
        if k < 2:
            halos[1][4 + k].send_on()

    from_dn = (BEHIND * AHEAD) * has_dn.astype(F32)
    from_up = (BEHIND * AHEAD) * has_up.astype(F32)

    def second(p):
        rows1(p).wait_recv()
        for i in range(2):
            planes = [plane(c1[p, i, pl.ds(4 * x, 4)]) for x in range(3)]
            fresh = advance(
                i, planes, lambda x: p51[p, i, pl.ds(4 * x, 4)],
                lambda x: yr1[0, p, pl.ds(3 * i + x, 1), :], lambda x: yr1[1, p, pl.ds(3 * i + x, 1), :],
            )
            fresh[0] = fresh[0] + from_dn * plane(sv[p, i, pl.ds(0, 4)])
            fresh[2] = fresh[2] + from_up * plane(sv[p, i, pl.ds(8, 4)])
            force_now = forcing(p, i, gp[1, i])
            for x in range(3):
                out[p, i, pl.ds(4 * x, 4)] = fresh[x].reshape(4, 8, 128) + force_now[4 * x : 4 * x + 4]

    loop(NP, second)

    rows1(NP).wait_recv()
    for i in range(2):
        planes = [plane(s1[pl.ds(i * NB + 4 * x, 4)]) for x in range(3)]
        fresh = advance(
            i, planes, lambda x: s1[pl.ds(at(7 + 6 * i) + 4 * x, 4)],
            lambda x: yr1[0, NP, pl.ds(3 * i + x, 1), :], lambda x: yr1[1, NP, pl.ds(3 * i + x, 1), :],
        )
        fresh[0] = fresh[0] + from_dn * plane(s0[pl.ds(i * NB, 4)])
        fresh[2] = fresh[2] + from_up * plane(s0[pl.ds(i * NB + 8, 4)])
        for x in range(3):
            s2[pl.ds(i * NB + 4 * x, 4)] = fresh[x].reshape(4, 8, 128)
    partial_state.wait_recv()
    merged = jnp.where(lane16 < 64, rrecv[0], rrecv[1])
    rolled = pltpu.roll(merged, 64, 1)
    for g in range(11):
        turn[...] = s2[pl.ds(16 * g, 16)].reshape(128, 128).T
        own = turn[pl.ds(mine, 16), :]
        if g == 0:
            own = own + jnp.where(lane16 < 32, BEHIND * merged, 0.0)
            own = own + jnp.where(lane16 >= 96, BEHIND * rolled, jnp.where(lane16 >= 64, AHEAD * merged, 0.0))
        if g == 1:
            own = own + jnp.where((lane16 >= 32) & (lane16 < 64), AHEAD * rolled, 0.0)
        for k in range(4):
            if 4 * g + k < 42:
                st_out[order[4 * g + k]] = own[:, 32 * k : 32 * k + 32]

    def last(p):
        for i in range(2):
            out[p, i, pl.ds(0, 4)] = out[p, i, pl.ds(0, 4)] + BEHIND * hx1[0, p, i]
            out[p, i, pl.ds(8, 4)] = out[p, i, pl.ds(8, 4)] + AHEAD * hx1[1, p, i]

    halo_state.wait_send()
    rows0.wait_send()
    rows0s.wait_send()
    for halo in halos[0]:
        halo.wait_send()
    loop(NP + 1, lambda q: rows1(q).wait_send())
    for gather in sets:
        gather.wait_send()

    for k in range(CHUNKS):
        halos[1][k].wait_recv()
        last(k)
    for halo in halos[1]:
        halo.wait_send()
    partial_state.wait_send()


def write_out(st, sens, st_out, out, sems):
    copies = [pltpu.make_async_copy(st, st_out, sems.at[NP])]
    copies += [pltpu.make_async_copy(sens.at[p], out.at[p], sems.at[p]) for p in range(NP)]
    for copy in copies:
        copy.start()
    for copy in copies:
        copy.wait()


def shards(state, sensitivity, packing, cell_zone, coefficients, param_target):
    packed = jnp.transpose(state, (0, 1, 3, 2)).reshape(42, 16, 32)
    vmem = pl.BlockSpec(memory_space=pltpu.VMEM)
    hbm = pl.BlockSpec(memory_space=pltpu.HBM)
    anywhere = pl.BlockSpec(memory_space=pl.ANY)
    scratch = [
        (NP, 14, NB, 8, 128),
        (NG, 128, 128),
        (16, 128), (2, 16, 128),
        (16, 128), (2, 16, 128), (128, 128),
        (192, 8, 128), (168, 8, 128), (176, 8, 128),
        (NB, 8, 8, 128), (NB, 10, 8, 128), (2, NB, 8, 128), (2, NB, 8, 128),
        (2, NB, 12, 8, 128), (2, NB, 12, 8, 128), (2, NB, 8, 12, 8, 128),
        (2, 2, NB, 8, 128),
        (2, NP, 2, 4, 8, 128), (2, NP, 2, 4, 8, 128), (2, VIA, 2, 4, 8, 128),
        (NP, 2, NB, 8, 128), (16, 8, 128), (NP, 2, NB, 8, 128), (NP, 2, NB, 8, 128),
        (2, NP + 1, 8, 128), (2, NP + 1, 8, 128), (2, NP + 1, 8, 128), (2, NP + 1, 8, 128),
        (42, 16, 32), (NB, 8, 128),
    ]
    new_state, new_sens = pl.pallas_call(
        kernel,
        out_shape=(
            jax.ShapeDtypeStruct((42, 16, 32), F32),
            jax.ShapeDtypeStruct((NP, 14, NB, 8, 128), F32),
        ),
        in_specs=[hbm] * 6,
        out_specs=(vmem, vmem),
        scratch_shapes=[pltpu.VMEM(shape, F32) for shape in scratch]
        + [
            pltpu.VMEM((NB, 8, 128), jnp.int32),
            pltpu.SMEM((8, 8), F32),
            pltpu.SMEM((NP,), jnp.int32),
            pltpu.SemaphoreType.DMA((MESSAGES,)),
            pltpu.SemaphoreType.DMA((MESSAGES,)),
            pltpu.SemaphoreType.DMA((LOCAL,)),
        ],
        compiler_params=pltpu.CompilerParams(
            collective_id=0, has_side_effects=True, vmem_limit_bytes=46 * 1024 * 1024
        ),
        name="column",
    )(
        *(
            pltpu.with_memory_space_constraint(x, pltpu.HBM)
            for x in (
                packed,
                sensitivity.reshape(NP, 14, NB, 8, 128),
                packing.reshape(NB, 8, 128),
                cell_zone.reshape(NB, 8, 128),
                coefficients,
                param_target,
            )
        )
    )
    new_state, new_sens = pl.pallas_call(
        write_out,
        out_shape=(
            jax.ShapeDtypeStruct((42, 16, 32), F32),
            jax.ShapeDtypeStruct((NP, 14, NB, 8, 128), F32),
        ),
        in_specs=[anywhere, anywhere],
        out_specs=(hbm, hbm),
        scratch_shapes=[pltpu.SemaphoreType.DMA((NP + 1,))],
        compiler_params=pltpu.CompilerParams(vmem_limit_bytes=2 * 1024 * 1024),
        name="write_out",
    )(new_state, new_sens)
    new_state = jnp.transpose(new_state.reshape(14, 3, 16, 32), (0, 1, 3, 2))
    return new_state, new_sens.reshape(NP, 14, 3, 32, 128)


def solution(mesh):
    placed = (
        P(None, "slab", "tile", "param"),
        P("param", None, "slab", "tile", None),
        P("slab", "tile", None),
        P("slab", "tile", None),
        P(),
        P("param"),
    )
    return jax.shard_map(
        shards,
        mesh=mesh,
        in_specs=placed,
        out_specs=(P(None, "slab", "tile", "param"), P("param", None, "slab", "tile", None)),
        check_vma=False,
    )
```

```python
import jax
import jax.numpy as jnp
from jax import lax
from jax.experimental import pallas as pl
from jax.experimental.pallas import tpu as pltpu
from jax.sharding import PartitionSpec as P

DT = 0.15
AHEAD = DT * 0.5
BEHIND = DT * 1.5
SIDE = DT * 0.25
CENTER = 1.0 - DT * 3.0
FILM = DT * 1.5
G = (0.3, 0.6, 0.9, 1.2, 1.5)
F32 = jnp.float32

NP = 8
NB = 12
NG = 12
ORDER = (0, 1, 7, 13, 2, 3, 4, 5, 6, 8, 9, 10, 11, 12)
SETS = ((0, 8), (8, 4))
CHUNKS = 8
VIA = 6

X0 = 0
X1 = X0 + 2 * CHUNKS
HS = X1 + 2 * CHUNKS
RS = HS + 2
Y0 = RS + 2
Y0S = Y0 + 2
Y1 = Y0S + 2
GATHER = Y1 + 18
RELAY = GATHER + 9 * len(SETS)
MESSAGES = RELAY + 2 * VIA
SMALL = NP + 1
LOCAL = SMALL + 5


def at(field):
    return ORDER.index(field) * NB


def kernel(
    st_arg, sens, pack_arg, zone_arg, coef_arg, targ_arg, st_out, out,
    sv, gst, hsend, hrecv, rsend, rrecv, turn,
    s0, s1, s2, th, ev, kv, pc, av, bv, gv, gp,
    hx0, hx1, relayed, bb, bs, c1, p51, yb0, yr0, yb1, yr1,
    st_in, pack, zone, coef, targ,
    ss, rs, lsem,
):
    me, sl, ti = (lax.axis_index(a) for a in ("param", "slab", "tile"))
    h, c = lax.div(me, 2), lax.rem(me, 2)
    jp = lax.rem(h + 1, 4) * 2 + c
    jm = lax.rem(h + 3, 4) * 2 + c
    jo = lax.rem(h + 2, 4) * 2 + c
    other = 1 - 2 * c
    has_dn, has_up = sl > 0, sl < 7
    has_lo, has_hi = ti > 0, ti < 3
    up, dn = (me, sl + 1, ti), (me, sl - 1, ti)
    hi, lo = (me, sl, ti + 1), (me, sl, ti - 1)
    right, left, sib = (jp, sl, ti), (jm, sl, ti), (me + other, sl, ti)
    up2, dn2 = (me, sl + 2, ti), (me, sl - 2, ti)
    has_dn2, has_up2 = sl > 1, sl < 6
    half, odd = lax.div(sl, 2), lax.rem(sl, 2) == 1
    relay_up = jnp.where(odd & has_up, 2 * half + 2, 0)
    relay_dn = jnp.where(jnp.logical_not(odd) & has_dn, 8 - 2 * half, 0)
    relay_here = jnp.where(odd, 2 * half, jnp.maximum(6 - 2 * half, 0))

    def loop(n, body):
        lax.fori_loop(0, n, lambda i, carry: (body(i), carry)[1], 0)

    def remote(src, dst, number, device, recv_number=None):
        recv_number = number if recv_number is None else recv_number
        return pltpu.make_async_remote_copy(
            src_ref=src, dst_ref=dst, send_sem=ss.at[number], recv_sem=rs.at[recv_number],
            device_id=device, device_id_type=pl.DeviceIdType.MESH,
        )

    barrier = pltpu.get_barrier_semaphore()

    def greet(device):
        pl.semaphore_signal(barrier, inc=1, device_id=device, device_id_type=pl.DeviceIdType.MESH)

    for device in (right, left, sib):
        greet(device)
    others = (
        (has_up, up), (has_dn, dn), (has_hi, hi), (has_lo, lo), (has_up2, up2), (has_dn2, dn2),
    )
    for present, device in others:
        pl.when(present)(lambda device=device: greet(device))
    present_count = sum(present.astype(jnp.int32) for present, _ in others)

    bulk_copy = pltpu.make_async_copy(sens.at[:, pl.ds(0, 2)], sv.at[:, pl.ds(0, 2)], lsem.at[NP])

    def shell_copy(p):
        return pltpu.make_async_copy(
            sens.at[p, pl.ds(2, 12)], sv.at[p, pl.ds(2, 12)], lsem.at[p]
        )

    small = [
        pltpu.make_async_copy(src, dst, lsem.at[SMALL + k])
        for k, (src, dst) in enumerate(
            ((st_arg, st_in), (pack_arg, pack), (zone_arg, zone), (coef_arg, coef), (targ_arg, targ))
        )
    ]
    for copy in small:
        copy.start()
    small[0].wait()
    mine = pl.multiple_of(me * 16, 16)
    order = [3 * field + x for field in ORDER for x in range(3)]

    def pack_group(planes):
        blank = jnp.zeros((16, 32), F32)
        return jnp.concatenate([blank if q is None else st_in[q] for q in planes], axis=-1)

    def pack_set(n):
        for g in range(SETS[n][0], min(SETS[n][0] + SETS[n][1], 11)):
            gst[g, pl.ds(mine, 16), :] = pack_group((order + [None] * 2)[4 * g : 4 * g + 4])

    pack_set(0)
    hsend[...] = pack_group((2, 5, 0, 3))

    pl.semaphore_wait(barrier, 3 + present_count)

    class Pair:
        def __init__(self, number, srcs, dsts, slab):
            plus, minus = (up, dn) if slab else (hi, lo)
            self.to_plus, self.to_minus = (has_up, has_dn) if slab else (has_hi, has_lo)
            self.a = remote(srcs[0], dsts[0], number, plus)
            self.b = remote(srcs[1], dsts[1], number + 1, minus)

        def start(self):
            pl.when(self.to_plus)(lambda: self.a.start())
            pl.when(self.to_minus)(lambda: self.b.start())

        def wait_recv(self):
            pl.when(self.to_minus)(lambda: self.a.wait_recv())
            pl.when(self.to_plus)(lambda: self.b.wait_recv())

        def wait_send(self):
            pl.when(self.to_plus)(lambda: self.a.wait_send())
            pl.when(self.to_minus)(lambda: self.b.wait_send())

    halo_state = Pair(HS, (hsend, hsend), (hrecv.at[0], hrecv.at[1]), True)

    class Halo:
        def __init__(self, n, k, srcs):
            base, target = ((X0, hx0), (X1, hx1))[n]
            dsts = [target.at[d, k] for d in range(2)]
            self.direct = Pair(base + 2 * k, srcs, dsts, True)
            self.k = k
            if k < VIA:
                slot, arrival = relayed.at[n, k], RELAY + VIA * n + k
                self.far = (
                    remote(srcs[0], slot, base + 2 * k, up2, arrival),
                    remote(srcs[1], slot, base + 2 * k + 1, dn2, arrival),
                )
                self.on = (
                    remote(slot, dsts[0], arrival, dn, base + 2 * k),
                    remote(slot, dsts[1], arrival, up, base + 2 * k + 1),
                )

        def start(self):
            ways = ((has_up, relay_up, self.direct.a), (has_dn, relay_dn, self.direct.b))
            for d, (present, count, copy) in enumerate(ways):
                pl.when(present & (self.k >= count))(lambda copy=copy: copy.start())
                if self.k < VIA:
                    pl.when(self.k < count)(lambda d=d: self.far[d].start())

        def send_on(self):
            @pl.when(self.k < relay_here)
            def _():
                self.far[0].wait_recv()
                pl.when(odd)(lambda: self.on[0].start())
                pl.when(jnp.logical_not(odd))(lambda: self.on[1].start())

        def wait_recv(self):
            self.direct.wait_recv()

        def wait_send(self):
            self.direct.wait_send()
            if self.k < VIA:
                pl.when(self.k < relay_here)(lambda: self.on[0].wait_send())

    def halo0(k):
        bulk = pl.ds(0, 2)
        return Halo(0, k, (sens.at[k, bulk, pl.ds(8, 4)], sens.at[k, bulk, pl.ds(0, 4)]))

    def halo1(k):
        return Halo(1, k, (bb.at[k, :, pl.ds(8, 4)], bb.at[k, :, pl.ds(0, 4)]))

    halos = [[halo0(k) for k in range(CHUNKS)], [halo1(k) for k in range(CHUNKS)]]
    partial_state = Pair(RS, (rsend, rsend), (rrecv.at[0], rrecv.at[1]), True)
    eight = pl.ds(0, NP)
    rows0 = Pair(Y0, (yb0.at[0, eight], yb0.at[1, eight]), (yr0.at[0, eight], yr0.at[1, eight]), False)

    def rows1(q):
        return Pair(Y1 + 2 * q, (yb1.at[0, q], yb1.at[1, q]), (yr1.at[0, q], yr1.at[1, q]), False)

    def shard(j, first, count):
        return gst.at[pl.ds(first, count), pl.ds(j * 16, 16)]

    rows0s = Pair(Y0S, (yb0.at[0, NP], yb0.at[1, NP]), (yr0.at[0, NP], yr0.at[1, NP]), False)

    class Gather:
        def __init__(self, first, count, number):
            def messages(shards):
                upper = count // 2
                whole, a, b = (first, count), (first, count - upper), (first + count - upper, upper)
                parts = (whole, whole, whole, a, whole, b, whole, a, b)
                devices = (right, left, sib, right, sib, left, sib, sib, sib)
                result = []
                for k in range(9):
                    ref = shard(shards[k], *parts[k])
                    result.append(remote(ref, ref, number + k, devices[k]))
                return result

            self.sent = messages((me, me, me, jm, jm, jp, jp, jo, jo))
            self.heard = messages(
                (jm, jp, me + other, jo, jm + other, jo, jp + other, jo + other, jo + other)
            )

        def start(self):
            for k in range(3):
                self.sent[k].start()

        def second(self):
            for k in range(2):
                self.heard[k].wait_recv()
                self.sent[3 + 2 * k].start()
                self.sent[4 + 2 * k].start()

        def third(self):
            for k in range(2):
                self.heard[3 + 2 * k].wait_recv()
                self.sent[7 + k].start()

        def finish(self):
            for k in (2, 4, 6, 7, 8):
                self.heard[k].wait_recv()

        def wait_send(self):
            for message in self.sent:
                message.wait_send()

    sets = [Gather(first, count, GATHER + 9 * n) for n, (first, count) in enumerate(SETS)]

    halo_state.start()
    sets[0].start()
    bulk_copy.start()
    loop(NP, lambda p: shell_copy(p).start())
    pack_set(1)

    def zero_tables(b):
        nothing = jnp.zeros((8, 128), F32)
        for n in range(2):
            for k in range(6):
                for f in range(12):
                    if k < 2 and f == 6 * k + 5 or k >= 2 and f // 6 == k % 2:
                        continue
                    gv[n, b, k, f] = nothing

    loop(NB, zero_tables)
    for copy in small[1:]:
        copy.wait()

    def clear(ref, k):
        ref[k] = jnp.zeros(ref.shape[1:], F32)

    for absent, k in ((jnp.logical_not(has_dn), 0), (jnp.logical_not(has_up), 1)):
        @pl.when(absent)
        def _(k=k):
            for ref in (hrecv, rrecv):
                clear(ref, k)
            def one(p):
                hx0[k, p] = jnp.zeros(hx0.shape[2:], F32)
                hx1[k, p] = jnp.zeros(hx1.shape[2:], F32)
            loop(NP, one)
    for absent, k in ((jnp.logical_not(has_lo), 0), (jnp.logical_not(has_hi), 1)):
        @pl.when(absent)
        def _(k=k):
            for ref in (yr0, yr1):
                clear(ref, k)

    def cell_theta(b):
        z = zone[b]
        is_zone = [z == j for j in range(1, 8)]
        values = []
        for k in range(8):
            v = jnp.full((8, 128), coef[k, 0], F32)
            for j in range(1, 8):
                v = jnp.where(is_zone[j - 1], coef[k, j], v)
            th[b, k] = v
            values.append(v)
        for i in range(2):
            exchange = DT * values[i] * pack[b]
            kv[i, b] = exchange
            pc[i, b] = CENTER - exchange
            for s in range(5):
                ev[b, 5 * i + s] = (DT * G[s]) * values[2 + i]

    loop(NB, cell_theta)

    bulk_copy.wait()

    def pack_rows0(p):
        for i in range(2):
            for x in range(3):
                r = 3 * i + x
                yb0[0, p, pl.ds(r, 1), :] = sv[p, i, 4 * x + 3, pl.ds(7, 1), :]
                yb0[1, p, pl.ds(r, 1), :] = sv[p, i, 4 * x, pl.ds(0, 1), :]

    loop(NP, pack_rows0)
    rows0.start()

    row = lax.broadcasted_iota(jnp.int32, (32, 128), 0)
    lane = lax.broadcasted_iota(jnp.int32, (32, 128), 1)

    def around(v, below, above):
        return (
            jnp.where(row == 0, below, pltpu.roll(v, 1, 0))
            + jnp.where(row == 31, above, pltpu.roll(v, 31, 0))
            + jnp.where(lane == 0, 0.0, pltpu.roll(v, 1, 1))
            + jnp.where(lane == 127, 0.0, pltpu.roll(v, 127, 1))
        )

    def plane(values):
        return values.reshape(32, 128)

    def advance(i, planes, outer, below, above):
        result = []
        for x in range(3):
            four = pl.ds(4 * x, 4)
            v = planes[x]
            w = plane(pc[i, four]) * v + plane(kv[i, four]) * plane(outer(x)) + SIDE * around(v, below(x), above(x))
            if x > 0:
                w = w + BEHIND * planes[x - 1]
            if x < 2:
                w = w + AHEAD * planes[x + 1]
            result.append(w)
        return result

    def forcing(p, i, values):
        t = targ[p]
        target = jnp.where(lax.div(t, 8) == i, lax.rem(t, 8), -1)
        return jnp.where(zone[...] == target, values, 0.0)

    def partial(p):
        shell_copy(p).wait()
        for i in range(2):
            planes = [plane(sv[p, i, pl.ds(4 * x, 4)]) for x in range(3)]
            fresh = advance(
                i, planes, lambda x: sv[p, 7 + 6 * i, pl.ds(4 * x, 4)],
                lambda x: yr0[0, p, pl.ds(3 * i + x, 1), :], lambda x: yr0[1, p, pl.ds(3 * i + x, 1), :],
            )
            for x in range(3):
                bb[p, i, pl.ds(4 * x, 4)] = fresh[x].reshape(4, 8, 128)

    lane16 = lax.broadcasted_iota(jnp.int32, (16, 128), 1)
    halo_state.wait_recv()
    gst[NG - 1, pl.ds(mine, 16), :] = jnp.where(lane16 < 64, hrecv[0], hrecv[1])
    sets[1].start()
    halos[0][0].start()
    sets[0].second()
    halos[0][1].start()
    sets[1].second()
    halos[0][2].start()
    halos[0][3].start()
    halos[0][4].start()
    halos[0][5].start()
    halos[0][6].start()
    halos[0][7].start()
    rows0.wait_recv()
    loop(NP, partial)
    for gather in sets:
        gather.third()
    for gather in sets:
        gather.finish()

    def unpack(g):
        s0[pl.ds(16 * g, 16)] = gst[g].T.reshape(16, 8, 128)

    def bulk_forcing(n, state, first, count):
        for i in range(2):
            gap = state[pl.ds(i * NB + first, count)] - state[pl.ds((2 + i) * NB + first, count)]
            gp[n, i, pl.ds(first, count)] = -(DT * pack[pl.ds(first, count)]) * gap

    def state_rows(state, buffer):
        for i in range(2):
            for x in range(3):
                r = 3 * i + x
                buffer[0, NP, pl.ds(r, 1), :] = state[i * NB + 4 * x + 3, pl.ds(7, 1), :]
                buffer[1, NP, pl.ds(r, 1), :] = state[i * NB + 4 * x, pl.ds(0, 1), :]

    loop(NG, unpack)
    state_rows(s0, yb0)
    rows0s.start()
    bulk_forcing(0, s0, 0, NB)
    for k in range(VIA):
        halos[0][k].send_on()
    def force(p):
        for i in range(2):
            bb[p, i] = bb[p, i] + forcing(p, i, gp[0, i])

    for k in range(6):
        force(k)
        halos[1][k].start()


    def tables(n, now, later):
        def block(b):
            kf, dp, qm, bb_ = ([th[b, 2 * k + i] for i in range(2)] for k in range(4))
            conc = [now[i * NB + b] for i in range(2)]
            pore = [[now[at(2 + 6 * i + s) + b] for s in range(6)] for i in range(2)]
            cap = [qm[i] * bb_[i] for i in range(2)]
            film = [FILM * kf[i] for i in range(2)]
            for s in range(6):
                inverse = 1.0 / (1.0 + bb_[0] * pore[0][s] + bb_[1] * pore[1][s])
                u = [pore[i][s] * inverse for i in range(2)]
                for i in range(2):
                    f = 6 * i + s
                    rate = DT * cap[i] * inverse
                    kept = 1.0 - bb_[i] * u[i]
                    own = 1.0 - rate * kept
                    if s == 5:
                        own = own - film[i]
                    av[n, b, 6 * i + s] = own
                    bv[n, b, 6 * i + s] = rate * u[i] * bb_[1 - i]
                    if s == 0:
                        flux = G[0] * (pore[i][1] - pore[i][0])
                    elif s == 5:
                        flux = -(G[4] * (pore[i][5] - pore[i][4]))
                    else:
                        flux = G[s] * (pore[i][s + 1] - pore[i][s]) - G[s - 1] * (pore[i][s] - pore[i][s - 1])
                    gv[n, b, 2 + i, f] = DT * flux
                    gv[n, b, 4 + i, f] = -(DT * bb_[i]) * u[i]
                    gv[n, b, 6 + i, f] = -(DT * qm[i]) * u[i] * kept
                    gv[n, b, 7 - i, f] = rate * pore[1 - i][s] * u[i]
                    fresh = pore[i][s] + DT * dp[i] * flux - DT * cap[i] * u[i]
                    if s == 5:
                        gap = conc[i] - pore[i][5]
                        gv[n, b, i, f] = FILM * gap
                        fresh = fresh + film[i] * gap
                    later[at(2 + f) + b] = fresh

        loop(NB, block)

    tables(0, s0, s1)

    rows0s.wait_recv()
    for i in range(2):
        planes = [plane(s0[pl.ds(i * NB + 4 * x, 4)]) for x in range(3)]
        fresh = advance(
            i, planes, lambda x: s0[pl.ds(at(7 + 6 * i) + 4 * x, 4)],
            lambda x: yr0[0, NP, pl.ds(3 * i + x, 1), :], lambda x: yr0[1, NP, pl.ds(3 * i + x, 1), :],
        )
        bs[pl.ds(4 * i, 4)] = fresh[2].reshape(4, 8, 128)
        bs[pl.ds(8 + 4 * i, 4)] = fresh[0].reshape(4, 8, 128)
        s1[pl.ds(i * NB, 4)] = fresh[0].reshape(4, 8, 128) + BEHIND * s0[pl.ds(176 + 4 * i, 4)]
        s1[pl.ds(i * NB + 4, 4)] = fresh[1].reshape(4, 8, 128)
        s1[pl.ds(i * NB + 8, 4)] = fresh[2].reshape(4, 8, 128) + AHEAD * s0[pl.ds(184 + 4 * i, 4)]
    state_rows(s1, yb1)
    rows1(NP).start()
    turn[...] = bs[...].reshape(128, 128).T
    rsend[...] = turn[pl.ds(mine, 16), :]
    partial_state.start()
    for k in range(6, CHUNKS):
        force(k)
        halos[1][k].start()
    halos[1][0].send_on()
    halos[1][1].send_on()
    bulk_forcing(1, s1, 0, NB)
    tables(1, s1, s2)
    halos[1][2].send_on()
    halos[1][3].send_on()

    def whole(p):
        for i in range(2):
            c1[p, i, pl.ds(0, 4)] = bb[p, i, pl.ds(0, 4)] + BEHIND * hx0[0, p, i]
            c1[p, i, pl.ds(4, 4)] = bb[p, i, pl.ds(4, 4)]
            c1[p, i, pl.ds(8, 4)] = bb[p, i, pl.ds(8, 4)] + AHEAD * hx0[1, p, i]
            for x in range(3):
                r = 3 * i + x
                yb1[0, p, pl.ds(r, 1), :] = c1[p, i, 4 * x + 3, pl.ds(7, 1), :]
                yb1[1, p, pl.ds(r, 1), :] = c1[p, i, 4 * x, pl.ds(0, 1), :]
        rows1(p).start()

    def shells(p):
        t = targ[p]
        kind, target_zone = lax.div(t, 8), lax.rem(t, 8)

        def block(b):
            within = zone[b] == target_zone
            t_now = [[sv[p, 2 + 6 * i + s, b] for s in range(6)] for i in range(2)]
            for n in range(2):
                bulk = sv if n == 0 else c1
                t_later = []
                for i in range(2):
                    flux = [ev[b, 5 * i + s] * (t_now[i][s + 1] - t_now[i][s]) for s in range(5)]
                    fresh = []
                    for s in range(6):
                        v = av[n, b, 6 * i + s] * t_now[i][s] + bv[n, b, 6 * i + s] * t_now[1 - i][s]
                        if s < 5:
                            v = v + flux[s]
                        if s > 0:
                            v = v - flux[s - 1]
                        if s == 5:
                            v = v + FILM * th[b, i] * bulk[p, i, b]
                        fresh.append(v + jnp.where(within, gv[n, b, kind, 6 * i + s], 0.0))
                    t_later.append(fresh)
                t_now = t_later
                if n == 0:
                    for i in range(2):
                        p51[p, i, b] = t_now[i][5]
            for i in range(2):
                for s in range(6):
                    out[p, 2 + 6 * i + s, b] = t_now[i][s]

        loop(NB, block)

    for k in range(4):
        for j in range(2):
            halos[0][2 * k + j].wait_recv()
            whole(2 * k + j)
        loop(2, lambda j: shells(2 * k + j))
        if k < 2:
            halos[1][4 + k].send_on()

    from_dn = (BEHIND * AHEAD) * has_dn.astype(F32)
    from_up = (BEHIND * AHEAD) * has_up.astype(F32)

    def second(p):
        rows1(p).wait_recv()
        for i in range(2):
            planes = [plane(c1[p, i, pl.ds(4 * x, 4)]) for x in range(3)]
            fresh = advance(
                i, planes, lambda x: p51[p, i, pl.ds(4 * x, 4)],
                lambda x: yr1[0, p, pl.ds(3 * i + x, 1), :], lambda x: yr1[1, p, pl.ds(3 * i + x, 1), :],
            )
            fresh[0] = fresh[0] + from_dn * plane(sv[p, i, pl.ds(0, 4)])
            fresh[2] = fresh[2] + from_up * plane(sv[p, i, pl.ds(8, 4)])
            force_now = forcing(p, i, gp[1, i])
            for x in range(3):
                out[p, i, pl.ds(4 * x, 4)] = fresh[x].reshape(4, 8, 128) + force_now[4 * x : 4 * x + 4]

    loop(NP, second)

    rows1(NP).wait_recv()
    for i in range(2):
        planes = [plane(s1[pl.ds(i * NB + 4 * x, 4)]) for x in range(3)]
        fresh = advance(
            i, planes, lambda x: s1[pl.ds(at(7 + 6 * i) + 4 * x, 4)],
            lambda x: yr1[0, NP, pl.ds(3 * i + x, 1), :], lambda x: yr1[1, NP, pl.ds(3 * i + x, 1), :],
        )
        fresh[0] = fresh[0] + from_dn * plane(s0[pl.ds(i * NB, 4)])
        fresh[2] = fresh[2] + from_up * plane(s0[pl.ds(i * NB + 8, 4)])
        for x in range(3):
            s2[pl.ds(i * NB + 4 * x, 4)] = fresh[x].reshape(4, 8, 128)
    partial_state.wait_recv()
    merged = jnp.where(lane16 < 64, rrecv[0], rrecv[1])
    rolled = pltpu.roll(merged, 64, 1)
    for g in range(11):
        turn[...] = s2[pl.ds(16 * g, 16)].reshape(128, 128).T
        own = turn[pl.ds(mine, 16), :]
        if g == 0:
            own = own + jnp.where(lane16 < 32, BEHIND * merged, 0.0)
            own = own + jnp.where(lane16 >= 96, BEHIND * rolled, jnp.where(lane16 >= 64, AHEAD * merged, 0.0))
        if g == 1:
            own = own + jnp.where((lane16 >= 32) & (lane16 < 64), AHEAD * rolled, 0.0)
        for k in range(4):
            if 4 * g + k < 42:
                st_out[order[4 * g + k]] = own[:, 32 * k : 32 * k + 32]

    def last(p):
        for i in range(2):
            out[p, i, pl.ds(0, 4)] = out[p, i, pl.ds(0, 4)] + BEHIND * hx1[0, p, i]
            out[p, i, pl.ds(8, 4)] = out[p, i, pl.ds(8, 4)] + AHEAD * hx1[1, p, i]

    halo_state.wait_send()
    rows0.wait_send()
    rows0s.wait_send()
    for halo in halos[0]:
        halo.wait_send()
    loop(NP + 1, lambda q: rows1(q).wait_send())
    for gather in sets:
        gather.wait_send()

    for k in range(CHUNKS):
        halos[1][k].wait_recv()
        last(k)
    for halo in halos[1]:
        halo.wait_send()
    partial_state.wait_send()


def write_out(st, sens, st_out, out, sems):
    copies = [pltpu.make_async_copy(st, st_out, sems.at[NP])]
    copies += [pltpu.make_async_copy(sens.at[p], out.at[p], sems.at[p]) for p in range(NP)]
    for copy in copies:
        copy.start()
    for copy in copies:
        copy.wait()


def shards(state, sensitivity, packing, cell_zone, coefficients, param_target):
    packed = jnp.transpose(state, (0, 1, 3, 2)).reshape(42, 16, 32)
    vmem = pl.BlockSpec(memory_space=pltpu.VMEM)
    hbm = pl.BlockSpec(memory_space=pltpu.HBM)
    anywhere = pl.BlockSpec(memory_space=pl.ANY)
    scratch = [
        (NP, 14, NB, 8, 128),
        (NG, 128, 128),
        (16, 128), (2, 16, 128),
        (16, 128), (2, 16, 128), (128, 128),
        (192, 8, 128), (168, 8, 128), (176, 8, 128),
        (NB, 8, 8, 128), (NB, 10, 8, 128), (2, NB, 8, 128), (2, NB, 8, 128),
        (2, NB, 12, 8, 128), (2, NB, 12, 8, 128), (2, NB, 8, 12, 8, 128),
        (2, 2, NB, 8, 128),
        (2, NP, 2, 4, 8, 128), (2, NP, 2, 4, 8, 128), (2, VIA, 2, 4, 8, 128),
        (NP, 2, NB, 8, 128), (16, 8, 128), (NP, 2, NB, 8, 128), (NP, 2, NB, 8, 128),
        (2, NP + 1, 8, 128), (2, NP + 1, 8, 128), (2, NP + 1, 8, 128), (2, NP + 1, 8, 128),
        (42, 16, 32), (NB, 8, 128),
    ]
    new_state, new_sens = pl.pallas_call(
        kernel,
        out_shape=(
            jax.ShapeDtypeStruct((42, 16, 32), F32),
            jax.ShapeDtypeStruct((NP, 14, NB, 8, 128), F32),
        ),
        in_specs=[hbm] * 6,
        out_specs=(vmem, vmem),
        scratch_shapes=[pltpu.VMEM(shape, F32) for shape in scratch]
        + [
            pltpu.VMEM((NB, 8, 128), jnp.int32),
            pltpu.SMEM((8, 8), F32),
            pltpu.SMEM((NP,), jnp.int32),
            pltpu.SemaphoreType.DMA((MESSAGES,)),
            pltpu.SemaphoreType.DMA((MESSAGES,)),
            pltpu.SemaphoreType.DMA((LOCAL,)),
        ],
        compiler_params=pltpu.CompilerParams(
            collective_id=0, has_side_effects=True, vmem_limit_bytes=46 * 1024 * 1024
        ),
        name="column",
    )(
        *(
            pltpu.with_memory_space_constraint(x, pltpu.HBM)
            for x in (
                packed,
                sensitivity.reshape(NP, 14, NB, 8, 128),
                packing.reshape(NB, 8, 128),
                cell_zone.reshape(NB, 8, 128),
                coefficients,
                param_target,
            )
        )
    )
    new_state, new_sens = pl.pallas_call(
        write_out,
        out_shape=(
            jax.ShapeDtypeStruct((42, 16, 32), F32),
            jax.ShapeDtypeStruct((NP, 14, NB, 8, 128), F32),
        ),
        in_specs=[anywhere, anywhere],
        out_specs=(hbm, hbm),
        scratch_shapes=[pltpu.SemaphoreType.DMA((NP + 1,))],
        compiler_params=pltpu.CompilerParams(vmem_limit_bytes=2 * 1024 * 1024),
        name="write_out",
    )(new_state, new_sens)
    new_state = jnp.transpose(new_state.reshape(14, 3, 16, 32), (0, 1, 3, 2))
    return new_state, new_sens.reshape(NP, 14, 3, 32, 128)


def solution(mesh):
    placed = (
        P(None, "slab", "tile", "param"),
        P("param", None, "slab", "tile", None),
        P("slab", "tile", None),
        P("slab", "tile", None),
        P(),
        P("param"),
    )
    return jax.shard_map(
        shards,
        mesh=mesh,
        in_specs=placed,
        out_specs=(P(None, "slab", "tile", "param"), P("param", None, "slab", "tile", None)),
        check_vma=False,
    )
```
